128 devices in a mesh: row: 32 (over z, x, core), col: 4 (over y).
Axes of the slice: x: 4, y: 4, z: 4, core: 2. Of those that a mesh axis runs over, the one named last changes fastest.
Arguments:
- noise: float32 [8192, 4096], P('row'), may hold values from -16 to 16
- data: float32 [4096, 4096], P('col', 'row'), may hold values from -16 to 16
Outputs:
- targets: float32 [8192, 4096], P('row', 'col')
- noise_potential: float32 [8192], P('row')
- data_potential: float32 [4096], P('col')
The draws below stay inside these ranges and needn't reach their ends.
All inputs are finite; a program needn't handle non-finite values.
Results may differ from the reference program's by a relative error of at most 0.0003.
Values sent between devices are 32-bit elements; how exact they have to be, the bound alone decides.
No kernel may reach another device: no remote copies, remote signals or barrier semaphores. Data moves between devices by JAX's collectives and lax.ppermute only.
A program may use at most 128 MiB of HBM per device.

```python
import math
import jax
import jax.numpy as jnp
from jax import lax

D = 4096
ITERS = 4
N = 8192
M = 4096


def noise_field(key, lowest, highest):
    base = jnp.clip(jax.random.normal(jax.random.fold_in(key, 101), (N, D), jnp.float32), -8.0, 8.0)
    scales = jnp.exp(jax.random.uniform(jax.random.fold_in(key, 102), (N, 1), jnp.float32, math.log(lowest), math.log(highest)))
    return base * scales


def draw_noise(key, part):
    return noise_field(key, 1.0, 1.0)


def draw_data(key, part):
    key = jax.random.fold_in(key, 7)
    return jnp.clip(jax.random.normal(jax.random.fold_in(key, 1), (M, D), jnp.float32), -8.0, 8.0)


def setup_inputs(seed: int = 0) -> dict:
    splits = jax.random.split(jax.random.key(seed), 3)
    return {
        "noise": draw_noise(jax.random.fold_in(splits[2], 71), 0),
        "data": draw_data(jax.random.fold_in(splits[2], 71), 0),
    }


EPSILON = 0.02


def log_total(scores, axis):
    peak = jnp.max(scores, axis=axis, keepdims=True)
    total = jnp.sum(jnp.exp(scores - peak), axis=axis)
    return jnp.squeeze(peak, axis=axis) + jnp.log(total)


def reference(noise, data):
    noise_norm = jnp.sum(noise * noise, axis=1)
    data_norm = jnp.sum(data * data, axis=1)
    cross = jnp.dot(noise, data.T, precision=lax.Precision.HIGHEST, preferred_element_type=jnp.float32)
    cost = (noise_norm[:, None] + data_norm[None, :] - 2.0 * cross) / D
    data_potential = jnp.zeros((M,), jnp.float32)
    for step in range(ITERS):
        noise_potential = -EPSILON * math.log(N) - EPSILON * log_total((data_potential[None, :] - cost) / EPSILON, 1)
        data_potential = -EPSILON * math.log(M) - EPSILON * log_total((noise_potential[:, None] - cost) / EPSILON, 0)
    noise_potential = -EPSILON * math.log(N) - EPSILON * log_total((data_potential[None, :] - cost) / EPSILON, 1)
    weights = jnp.exp((noise_potential[:, None] + data_potential[None, :] - cost) / EPSILON) * N
    targets = jnp.dot(weights, data, precision=lax.Precision.HIGHEST, preferred_element_type=jnp.float32)
    return targets, noise_potential, data_potential
```

```python
import functools
import math

import jax
import jax.numpy as jnp
from jax import lax
from jax.experimental import pallas as pl
from jax.experimental.pallas import tpu as pltpu
from jax.sharding import PartitionSpec as P

ITERS = 4
EPSILON = 0.02
LOG2E = 1.0 / math.log(2.0)
SCALE = LOG2E / EPSILON
VMEM_LIMIT = 48 * 1024 * 1024


def split(v):
    hi = v.astype(jnp.bfloat16)
    return hi, (v - hi.astype(jnp.float32)).astype(jnp.bfloat16)


def dot3(a, b, dims):
    a_hi, a_lo = split(a)
    b_hi, b_lo = split(b)
    mul = functools.partial(
        lax.dot_general, dimension_numbers=(dims, ((), ())), preferred_element_type=jnp.float32
    )
    return mul(a_hi, b_hi) + (mul(a_hi, b_lo) + mul(a_lo, b_hi))


def cross_kernel(factor, noise_ref, data_ref, cross_ref, norm_ref, square_ref):
    step = pl.program_id(0)
    joined = jnp.concatenate([data_ref[0], data_ref[1]], axis=1)
    columns = pl.ds(pl.multiple_of(step * joined.shape[1], joined.shape[1]), joined.shape[1])
    product = dot3(noise_ref[:, columns], joined, ((1,), (1,)))
    squares = data_ref[0] * data_ref[0] + data_ref[1] * data_ref[1]

    @pl.when(step == 0)
    def _():
        cross_ref[...] = product
        square_ref[...] = squares

    @pl.when(step > 0)
    def _():
        cross_ref[...] += product
        square_ref[...] += squares

    @pl.when(step == pl.num_programs(0) - 1)
    def _():
        cross_ref[...] = cross_ref[...] * factor
        norm_ref[...] = lax.dot_general(
            jnp.ones((8, square_ref.shape[1]), jnp.float32),
            square_ref[...],
            (((1,), (1,)), ((), ())),
            precision=lax.Precision.HIGHEST,
            preferred_element_type=jnp.float32,
        )


def cross_products(noise, gathered):
    rows, width = noise.shape
    blocks, cols, part = gathered.shape
    return pl.pallas_call(
        functools.partial(cross_kernel, 2.0 * SCALE / width),
        grid=(blocks // 2,),
        in_specs=[
            pl.BlockSpec((rows, width), lambda s: (0, 0)),
            pl.BlockSpec((2, cols, part), lambda s: (s, 0, 0)),
        ],
        out_specs=[
            pl.BlockSpec((rows, cols), lambda s: (0, 0)),
            pl.BlockSpec((8, cols), lambda s: (0, 0)),
        ],
        out_shape=[
            jax.ShapeDtypeStruct((rows, cols), jnp.float32),
            jax.ShapeDtypeStruct((8, cols), jnp.float32),
        ],
        scratch_shapes=[pltpu.VMEM((cols, part), jnp.float32)],
        compiler_params=pltpu.CompilerParams(vmem_limit_bytes=VMEM_LIMIT),
        cost_estimate=pl.CostEstimate(
            flops=6 * rows * cols * width, bytes_accessed=4 * cols * width, transcendentals=0
        ),
    )(noise, gathered)


def target_kernel(
    place_ref,
    noise_ref,
    data_pot_ref,
    own_ref,
    left0_ref,
    left1_ref,
    right0_ref,
    right1_ref,
    far0_ref,
    far1_ref,
    data_ref,
    target_ref,
    total_ref,
    sums_ref,
):
    offset, quarter = pl.program_id(0), pl.program_id(1)
    depth = data_ref.shape[3]
    half = left0_ref.shape[0]
    peer = lax.rem(place_ref[0] + 4 - offset, 4)
    columns = pl.ds(pl.multiple_of(quarter * depth, depth), depth)
    values = jnp.concatenate([data_ref[0, b, 0] for b in range(data_ref.shape[1])], axis=1)
    data_hi, data_lo = split(values)

    @pl.when((offset == 0) & (quarter == 0))
    def _():
        target_ref[...] = jnp.zeros_like(target_ref)
        sums_ref[...] = jnp.zeros_like(sums_ref)

    def accumulate(refs):
        for part, ref in enumerate(refs):
            height = ref.shape[0]
            rows = pl.ds(part * height, height)
            score = ref[:, columns] + noise_ref[rows, :] + data_pot_ref[offset, :, columns]
            weight = jnp.exp2(score)
            folded = sum(weight[:, c : c + 128] for c in range(0, depth, 128))
            sums_ref[peer, rows, :] += folded
            w_hi, w_lo = split(weight)
            mul = functools.partial(jnp.dot, preferred_element_type=jnp.float32)
            target_ref[rows, :] += mul(w_hi, data_hi) + (mul(w_hi, data_lo) + mul(w_lo, data_hi))

    pieces = ((own_ref,), (left0_ref, left1_ref), (far0_ref, far1_ref), (right0_ref, right1_ref))
    for which, refs in enumerate(pieces):
        pl.when(offset == which)(functools.partial(accumulate, refs))

    @pl.when((offset == 3) & (quarter == 3))
    def _():
        total = (sums_ref[0] + sums_ref[1]) + (sums_ref[2] + sums_ref[3])
        total = jnp.sum(total, axis=1, keepdims=True)
        target_ref[...] = target_ref[...] / total
        total_ref[...] = jnp.broadcast_to(total, total_ref.shape)


def weighted_targets(place, noise_pot, data_pots, own, left, right, far, gathered):
    rows, cols = own.shape
    part = gathered.shape[-1]
    data = gathered.reshape(4, 8, 4, cols // 4, part)
    whole = lambda shape: pl.BlockSpec(shape, lambda o, q, place: (0,) * len(shape))
    half = (rows // 2, cols)
    return pl.pallas_call(
        target_kernel,
        grid_spec=pltpu.PrefetchScalarGridSpec(
            num_scalar_prefetch=1,
            grid=(4, 4),
            in_specs=[
                whole((rows, 1)),
                whole((4, 1, cols)),
                whole((rows, cols)),
                *[whole(half)] * 6,
                pl.BlockSpec(
                    (1, 8, 1, cols // 4, part),
                    lambda o, q, place: (q, 0, lax.rem(q + 4 - place[0] + o, 4), 0, 0),
                ),
            ],
            out_specs=[whole((rows, 8 * part)), whole((rows, 128))],
            scratch_shapes=[pltpu.VMEM((4, rows, 128), jnp.float32)],
        ),
        out_shape=[
            jax.ShapeDtypeStruct((rows, 8 * part), jnp.float32),
            jax.ShapeDtypeStruct((rows, 128), jnp.float32),
        ],
        compiler_params=pltpu.CompilerParams(vmem_limit_bytes=VMEM_LIMIT),
        cost_estimate=pl.CostEstimate(
            flops=24 * rows * cols * 8 * part, bytes_accessed=20 * 1024 * 1024, transcendentals=4 * rows * cols
        ),
    )(place, noise_pot, data_pots, own, *left, *right, *far, data)


def shift(v, by):
    return lax.ppermute(v, "col", [(i, (i + by) % 4) for i in range(4)])


def around(v):
    return shift(v, 1), shift(v, 2), shift(v, 3)


def spread(v):
    return lax.all_to_all(jnp.broadcast_to(v[None], (32,) + v.shape), "row", 0, 0, tiled=True)


def pair_logsum(peaks, totals):
    peak = functools.reduce(jnp.maximum, peaks)
    scaled = [t * jnp.exp2(p - peak) for p, t in zip(peaks, totals)]
    return peak + jnp.log2((scaled[0] + scaled[2]) + (scaled[1] + scaled[3]))


def local(noise, data):
    rows, width = noise.shape
    cols, part = data.shape
    rows_all, cols_all = rows * 32, cols * 4
    log_rows, log_cols = math.log2(rows_all), math.log2(cols_all)
    place = lax.axis_index("col")
    quarter = cols // 4

    pieces = []
    for k in range(4):
        block = lax.dynamic_slice(data, (lax.rem(place + k, 4) * quarter, 0), (quarter, part))
        pairs = []
        for z in range(4):
            for xc in range(8):
                for y in range(4):
                    pairs.append(((z * 8 + xc) * 4 + y, (((y + k) % 4) * 8 + xc) * 4 + z))
        pieces.append(lax.ppermute(block, ("row", "col"), pairs))
    turned = jnp.concatenate(pieces, axis=0)

    gathered = lax.all_gather(data, "row", axis=0, tiled=False)
    noise_norm = jnp.sum(noise * noise, axis=1) / width
    scores, norms = cross_products(noise, gathered)
    data_norm = norms[0] / width

    gathered, turned = lax.optimization_barrier((gathered, turned))
    turned = lax.all_gather(turned, "row", axis=0, tiled=False)

    shifted = scores - (data_norm * SCALE)[None, :]
    peak = jnp.max(shifted, axis=1)
    total = jnp.sum(jnp.exp2(shifted - peak[:, None]), axis=1)
    pair = jnp.stack([peak, total])
    pairs = (pair,) + around(pair)
    noise_pot = -log_rows - pair_logsum([p[0] for p in pairs], [p[1] for p in pairs])

    halves = (scores[: rows // 2], scores[rows // 2 :])
    shifted = scores + noise_pot[:, None]
    peak = jnp.max(shifted, axis=0)
    total = jnp.sum(jnp.exp2(shifted - peak[None, :]), axis=0)
    pair = jnp.concatenate([peak, total]).reshape(16, 128)
    pair, first = lax.optimization_barrier((pair, halves[0]))
    left0, right0 = shift(first, 1), shift(first, 3)
    pairs = spread(pair)
    pairs, left0, right0 = lax.optimization_barrier((pairs, left0, right0))
    peaks, totals = pairs[:, :8].reshape(32, cols), pairs[:, 8:].reshape(32, cols)
    peak = jnp.max(peaks, axis=0)
    total = jnp.sum(totals * jnp.exp2(peaks - peak[None, :]), axis=0)
    data_pot = -log_cols - (peak + jnp.log2(total))

    for step in range(1, ITERS):
        total = jnp.sum(jnp.exp2(scores + noise_pot[:, None] + data_pot[None, :]), axis=1)
        one, two, three = around(total)
        noise_pot = noise_pot - log_rows - jnp.log2((total + two) + (one + three))
        total = jnp.sum(jnp.exp2(scores + noise_pot[:, None] + data_pot[None, :]), axis=0)
        total = total.reshape(8, 128)
        if step == 1:
            total, second = lax.optimization_barrier((total, halves[1]))
            left1, right1 = shift(second, 1), shift(second, 3)
            totals = spread(total)
            totals, left1, right1 = lax.optimization_barrier((totals, left1, right1))
        elif step == 2:
            total, left0, right1 = lax.optimization_barrier((total, left0, right1))
            far0, far1 = shift(left0, 1), shift(right1, 3)
            totals = spread(total)
            totals, far0, far1 = lax.optimization_barrier((totals, far0, far1))
        else:
            totals = spread(total)
        data_pot = data_pot - log_cols - jnp.log2(jnp.sum(totals, axis=0).reshape(cols))

    data_pots = jnp.stack((data_pot,) + around(data_pot))[:, None, :]
    targets, total = weighted_targets(
        place.reshape(1).astype(jnp.int32),
        noise_pot[:, None],
        data_pots,
        scores,
        (left0, left1),
        (right0, right1),
        (far0, far1),
        turned,
    )
    noise_pot = noise_pot - log_rows - jnp.log2(total[:, 0])
    return (targets, noise_norm + noise_pot / SCALE, data_norm + data_pot / SCALE)


def solution(mesh):
    placed = (P("row", None), P("col", "row"))
    return jax.shard_map(
        local,
        mesh=mesh,
        in_specs=placed,
        out_specs=(P("row", "col"), P("row"), P("col")),
        check_vma=False,
    )
```

```python
import functools
import math

import jax
import jax.numpy as jnp
from jax import lax
from jax.experimental import pallas as pl
from jax.experimental.pallas import tpu as pltpu
from jax.sharding import PartitionSpec as P

ITERS = 4
EPSILON = 0.02
LOG2E = 1.0 / math.log(2.0)
SCALE = LOG2E / EPSILON
VMEM_LIMIT = 40 * 1024 * 1024


def split(v):
    hi = v.astype(jnp.bfloat16)
    return hi, (v - hi.astype(jnp.float32)).astype(jnp.bfloat16)


def split_kernel(value_ref, hi_ref, lo_ref):
    hi_ref[...], lo_ref[...] = split(value_ref[...])


def split_noise(noise):
    rows, width = noise.shape
    block = pl.BlockSpec((rows, 512), lambda i: (0, i))
    return pl.pallas_call(
        split_kernel,
        grid=(width // 512,),
        in_specs=[block],
        out_specs=[block] * 2,
        out_shape=[jax.ShapeDtypeStruct((rows, width), jnp.bfloat16)] * 2,
    )(noise)


def cross_kernel(factor, group, hi_ref, lo_ref, data_hbm, cross_ref, norm_ref, data_ref, square_ref, sems):
    blocks, cols, part = data_ref.shape
    depth = group * part
    copies = [
        pltpu.make_async_copy(
            data_hbm.at[pl.ds(i * group, group)], data_ref.at[pl.ds(i * group, group)], sems.at[i]
        )
        for i in range(blocks // group)
    ]
    for copy in copies:
        copy.start()
    for i, copy in enumerate(copies):
        copy.wait()
        values = [data_ref[i * group + j] for j in range(group)]
        joined = jnp.concatenate(values, axis=1)
        data_hi, data_lo = split(joined)
        columns = slice(i * depth, (i + 1) * depth)
        mul = functools.partial(
            lax.dot_general,
            dimension_numbers=(((1,), (1,)), ((), ())),
            preferred_element_type=jnp.float32,
        )
        noise_hi = hi_ref[:, columns]
        product = mul(noise_hi, data_hi) + (mul(noise_hi, data_lo) + mul(lo_ref[:, columns], data_hi))
        squares = sum(v * v for v in values)
        if i == 0:
            cross_ref[...] = product
            square_ref[...] = squares
        else:
            cross_ref[...] += product
            square_ref[...] += squares
    cross_ref[...] = cross_ref[...] * factor
    norm_ref[...] = lax.dot_general(
        jnp.ones((8, part), jnp.float32),
        square_ref[...],
        (((1,), (1,)), ((), ())),
        precision=lax.Precision.HIGHEST,
        preferred_element_type=jnp.float32,
    )


def cross_products(noise_hi, noise_lo, gathered):
    rows, width = noise_hi.shape
    blocks, cols, part = gathered.shape
    group = 4
    return pl.pallas_call(
        functools.partial(cross_kernel, 2.0 * SCALE / width, group),
        in_specs=[pl.BlockSpec(memory_space=pltpu.VMEM)] * 2 + [pl.BlockSpec(memory_space=pl.ANY)],
        out_specs=[pl.BlockSpec(memory_space=pltpu.VMEM)] * 2,
        out_shape=[
            jax.ShapeDtypeStruct((rows, cols), jnp.float32),
            jax.ShapeDtypeStruct((8, cols), jnp.float32),
        ],
        scratch_shapes=[
            pltpu.VMEM((blocks, cols, part), jnp.float32),
            pltpu.VMEM((cols, part), jnp.float32),
            pltpu.SemaphoreType.DMA((blocks // group,)),
        ],
        compiler_params=pltpu.CompilerParams(vmem_limit_bytes=VMEM_LIMIT),
        cost_estimate=pl.CostEstimate(
            flops=6 * rows * cols * width, bytes_accessed=4 * cols * width, transcendentals=0
        ),
    )(noise_hi, noise_lo, gathered)


def target_kernel(
    place_ref,
    noise_ref,
    data_pot_ref,
    own_ref,
    left0_hbm,
    left1_hbm,
    right0_hbm,
    right1_hbm,
    far0_hbm,
    far1_hbm,
    data_hbm,
    target_ref,
    total_ref,
    score_ref,
    data_ref,
    sums_ref,
    score_sems,
    data_sems,
):
    place = place_ref[0]
    depth = data_ref.shape[2]
    half = left0_hbm.shape[0]
    mul = functools.partial(jnp.dot, preferred_element_type=jnp.float32)
    pieces = ((left0_hbm, left1_hbm), (far0_hbm, far1_hbm), (right0_hbm, right1_hbm))
    score_copies, data_copies = [], []
    for offset in range(4):
        if offset:
            score_copies.append(
                [
                    pltpu.make_async_copy(
                        piece, score_ref.at[offset - 1, pl.ds(i * half, half)], score_sems.at[offset - 1, i]
                    )
                    for i, piece in enumerate(pieces[offset - 1])
                ]
            )
            for copy in score_copies[-1]:
                copy.start()
        for quarter in range(4):
            data_copies.append(
                pltpu.make_async_copy(
                    data_hbm.at[quarter, :, offset],
                    data_ref.at[offset * 4 + quarter],
                    data_sems.at[offset * 4 + quarter],
                )
            )
            data_copies[-1].start()
    for offset in range(4):
        if offset:
            for copy in score_copies[offset - 1]:
                copy.wait()
        folded = 0.0
        for quarter in range(4):
            step = offset * 4 + quarter
            data_copies[step].wait()
            columns = slice(quarter * depth, (quarter + 1) * depth)
            values = jnp.concatenate([data_ref[step, b] for b in range(data_ref.shape[1])], axis=1)
            data_hi, data_lo = split(values)
            scores = score_ref[offset - 1, :, columns] if offset else own_ref[:, columns]
            weight = jnp.exp2(scores + noise_ref[...] + data_pot_ref[offset, :, columns])
            folded += sum(weight[:, c : c + 128] for c in range(0, depth, 128))
            w_hi, w_lo = split(weight)
            product = mul(w_hi, data_hi) + (mul(w_hi, data_lo) + mul(w_lo, data_hi))
            if step == 0:
                target_ref[...] = product
            else:
                target_ref[...] += product
        sums_ref[lax.rem(place + 4 - offset, 4)] = folded
    total = (sums_ref[0] + sums_ref[1]) + (sums_ref[2] + sums_ref[3])
    total = jnp.sum(total, axis=1, keepdims=True)
    target_ref[...] = target_ref[...] / total
    total_ref[...] = jnp.broadcast_to(total, total_ref.shape)


def weighted_targets(place, noise_pot, data_pots, own, left, right, far, gathered):
    rows, cols = own.shape
    part = gathered.shape[-1]
    data = gathered.reshape(4, 8, 4, cols // 4, part)
    vmem, hbm = pl.BlockSpec(memory_space=pltpu.VMEM), pl.BlockSpec(memory_space=pl.ANY)
    return pl.pallas_call(
        target_kernel,
        in_specs=[pl.BlockSpec(memory_space=pltpu.SMEM)] + [vmem] * 3 + [hbm] * 7,
        out_specs=[vmem] * 2,
        out_shape=[
            jax.ShapeDtypeStruct((rows, 8 * part), jnp.float32),
            jax.ShapeDtypeStruct((rows, 128), jnp.float32),
        ],
        scratch_shapes=[
            pltpu.VMEM((3, rows, cols), jnp.float32),
            pltpu.VMEM((16, 8, cols // 4, part), jnp.float32),
            pltpu.VMEM((4, rows, 128), jnp.float32),
            pltpu.SemaphoreType.DMA((3, 2)),
            pltpu.SemaphoreType.DMA((16,)),
        ],
        compiler_params=pltpu.CompilerParams(vmem_limit_bytes=VMEM_LIMIT),
        cost_estimate=pl.CostEstimate(
            flops=24 * rows * cols * 8 * part, bytes_accessed=20 * 1024 * 1024, transcendentals=4 * rows * cols
        ),
    )(place, noise_pot, data_pots, own, *left, *right, *far, data)


def shift(v, by):
    return lax.ppermute(v, "col", [(i, (i + by) % 4) for i in range(4)])


def around(v):
    return shift(v, 1), shift(v, 2), shift(v, 3)


def spread(v):
    return lax.all_to_all(jnp.broadcast_to(v[None], (32,) + v.shape), "row", 0, 0, tiled=True)


def pair_logsum(peaks, totals):
    peak = functools.reduce(jnp.maximum, peaks)
    scaled = [t * jnp.exp2(p - peak) for p, t in zip(peaks, totals)]
    return peak + jnp.log2((scaled[0] + scaled[2]) + (scaled[1] + scaled[3]))


def local(noise, data):
    rows, width = noise.shape
    cols, part = data.shape
    rows_all, cols_all = rows * 32, cols * 4
    log_rows, log_cols = math.log2(rows_all), math.log2(cols_all)
    place = lax.axis_index("col")
    quarter = cols // 4

    gathered = lax.all_gather(data, "row", axis=0, tiled=False)

    blocks = data.reshape(4, quarter, part)
    level = lax.axis_index("row") // 8
    held = []
    for k in range(4):
        block = lax.dynamic_index_in_dim(blocks, lax.rem(level + k, 4), 0, keepdims=False)
        held.append(lax.ppermute(block, "row", [(i, (i + 8 * k) % 32) for i in range(32)]) if k else block)
    held = jnp.stack(held)
    turned = []
    for k in range(4):
        block = lax.dynamic_index_in_dim(held, lax.rem(level + 8 - place - k, 4), 0, keepdims=False)
        turned.append(shift(block, k) if k else block)
    turned = jnp.concatenate(turned, axis=0)

    noise_norm = jnp.sum(noise * noise, axis=1) / width
    parts = split_noise(noise)
    gathered, turned, parts, noise_norm = lax.optimization_barrier((gathered, turned, parts, noise_norm))
    scores, norms = cross_products(*parts, gathered)
    data_norm = norms[0] / width

    turned = lax.all_gather(turned, "row", axis=0, tiled=False)

    shifted = scores - (data_norm * SCALE)[None, :]
    peak = jnp.max(shifted, axis=1)
    total = jnp.sum(jnp.exp2(shifted - peak[:, None]), axis=1)
    pair = jnp.stack([peak, total])
    pairs = (pair,) + around(pair)
    noise_pot = -log_rows - pair_logsum([p[0] for p in pairs], [p[1] for p in pairs])

    halves = (scores[: rows // 2], scores[rows // 2 :])
    shifted = scores + noise_pot[:, None]
    peak = jnp.max(shifted, axis=0)
    total = jnp.sum(jnp.exp2(shifted - peak[None, :]), axis=0)
    pair = jnp.concatenate([peak, total]).reshape(16, 128)
    noise_pot, first = lax.optimization_barrier((noise_pot, halves[0]))
    left0, right0 = shift(first, 1), shift(first, 3)
    pairs = spread(pair)
    pairs, left0, right0 = lax.optimization_barrier((pairs, left0, right0))
    peaks, totals = pairs[:, :8].reshape(32, cols), pairs[:, 8:].reshape(32, cols)
    peak = jnp.max(peaks, axis=0)
    total = jnp.sum(totals * jnp.exp2(peaks - peak[None, :]), axis=0)
    data_pot = -log_cols - (peak + jnp.log2(total))

    for step in range(1, ITERS):
        total = jnp.sum(jnp.exp2(scores + noise_pot[:, None] + data_pot[None, :]), axis=1)
        one, two, three = around(total)
        noise_pot = noise_pot - log_rows - jnp.log2((total + two) + (one + three))
        total = jnp.sum(jnp.exp2(scores + noise_pot[:, None] + data_pot[None, :]), axis=0)
        total = total.reshape(8, 128)
        if step == 1:
            noise_pot, second = lax.optimization_barrier((noise_pot, halves[1]))
            left1, right1 = shift(second, 1), shift(second, 3)
            totals = spread(total)
            totals, left1, right1 = lax.optimization_barrier((totals, left1, right1))
        elif step == 2:
            noise_pot, left0, right1 = lax.optimization_barrier((noise_pot, left0, right1))
            far0, far1 = shift(left0, 1), shift(right1, 3)
            totals = spread(total)
            totals, far0, far1 = lax.optimization_barrier((totals, far0, far1))
        else:
            totals = spread(total)
        data_pot = data_pot - log_cols - jnp.log2(jnp.sum(totals, axis=0).reshape(cols))

    data_pots = jnp.stack((data_pot,) + around(data_pot))[:, None, :]
    targets, total = weighted_targets(
        place.reshape(1).astype(jnp.int32),
        noise_pot[:, None],
        data_pots,
        scores,
        (left0, left1),
        (right0, right1),
        (far0, far1),
        turned,
    )
    noise_pot = noise_pot - log_rows - jnp.log2(total[:, 0])
    return (targets, noise_norm + noise_pot / SCALE, data_norm + data_pot / SCALE)


def solution(mesh):
    placed = (P("row", None), P("col", "row"))
    return jax.shard_map(
        local,
        mesh=mesh,
        in_specs=placed,
        out_specs=(P("row", "col"), P("row"), P("col")),
        check_vma=False,
    )
```

```python
import functools
import math

import jax
import jax.numpy as jnp
from jax import lax
from jax.experimental import pallas as pl
from jax.experimental.pallas import tpu as pltpu
from jax.sharding import PartitionSpec as P

ITERS = 4
EPSILON = 0.02
LOG2E = 1.0 / math.log(2.0)
SCALE = LOG2E / EPSILON
VMEM_LIMIT = 40 * 1024 * 1024
PASSED = 512


def split(v):
    hi = v.astype(jnp.bfloat16)
    return hi, (v - hi.astype(jnp.float32)).astype(jnp.bfloat16)


def split_kernel(place_ref, own_hbm, other_hbm, hi_ref, lo_ref, held_ref, sems):
    rows, part = held_ref.shape[2:]
    copies = []
    for n in range(16):
        block = lax.rem(place_ref[0] + 4 - n // 4, 4) * 4 + lax.rem(place_ref[1] + 4 - n % 4, 4)
        columns = pl.ds(pl.multiple_of((block * 2 + place_ref[2]) * part, part), part)
        for i, noise in enumerate((own_hbm, other_hbm)):
            copies.append(pltpu.make_async_copy(noise.at[:, columns], held_ref.at[n, i], sems.at[n, i]))
            copies[-1].start()
    for n in range(16):
        for i in range(2):
            copies[2 * n + i].wait()
            hi, lo = split(held_ref[n, i])
            hi_ref[i * rows : (i + 1) * rows, n * part : (n + 1) * part] = hi
            lo_ref[i * rows : (i + 1) * rows, n * part : (n + 1) * part] = lo


def split_noise(place, own, other):
    rows, width = own.shape
    part = width // 32
    vmem, hbm = pl.BlockSpec(memory_space=pltpu.VMEM), pl.BlockSpec(memory_space=pltpu.HBM)
    return pl.pallas_call(
        split_kernel,
        in_specs=[pl.BlockSpec(memory_space=pltpu.SMEM), hbm, hbm],
        out_specs=[vmem] * 2,
        out_shape=[jax.ShapeDtypeStruct((2 * rows, 16 * part), jnp.bfloat16)] * 2,
        scratch_shapes=[pltpu.VMEM((16, 2, rows, part), jnp.float32), pltpu.SemaphoreType.DMA((16, 2))],
        compiler_params=pltpu.CompilerParams(vmem_limit_bytes=8 * 1024 * 1024),
        cost_estimate=pl.CostEstimate(flops=0, bytes_accessed=16 * 1024 * 1024, transcendentals=0),
    )(place, own, other)


def block_product(hi_ref, lo_ref, blocks, values):
    part = values[0].shape[1]
    pick = lambda ref: jnp.concatenate([ref[:, n * part : (n + 1) * part] for n in blocks], axis=1)
    noise_hi, noise_lo = pick(hi_ref), pick(lo_ref)
    data_hi, data_lo = split(jnp.concatenate(values, axis=1))
    mul = functools.partial(
        lax.dot_general, dimension_numbers=(((1,), (1,)), ((), ())), preferred_element_type=jnp.float32
    )
    return mul(noise_hi, data_hi) + (mul(noise_hi, data_lo) + mul(noise_lo, data_hi))


def ring_squares(values):
    return (values[0] * values[0] + values[2] * values[2]) + (values[1] * values[1] + values[3] * values[3])


def block_number(first, across, along):
    return across * 4 + along if first == "x" else along * 4 + across


def near_kernel(hi_ref, lo_ref, *refs):
    cross_ref, even_ref, odd_ref = refs[6:]
    for half, (first, lines) in enumerate((("x", refs[:3]), ("z", refs[3:6]))):
        cols = lines[0].shape[1]
        place = slice(half * cols, (half + 1) * cols)
        squares = []
        for line, across in zip(lines, (0, 1, 3)):
            values = [line[n] for n in range(4)]
            numbers = [block_number(first, across, n) for n in range(4)]
            product = block_product(hi_ref, lo_ref, numbers, values)
            if across == 0:
                cross_ref[:, place] = product
            else:
                cross_ref[:, place] += product
            squares.append(ring_squares(values))
        even_ref[place, :] = squares[0]
        odd_ref[place, :] = squares[1] + squares[2]


def far_kernel(factor, hi_ref, lo_ref, cross_ref, even_ref, odd_ref, x0, x1, z0, z1, own_ref, other_ref, norm_ref):
    rows = own_ref.shape[0]
    for half, (first, refs) in enumerate((("x", (x0, x1)), ("z", (z0, z1)))):
        cols = refs[0].shape[1]
        place = slice(half * cols, (half + 1) * cols)
        values = [refs[i // 2][i % 2] for i in range(4)]
        numbers = [block_number(first, 2, i) for i in range(4)]
        product = (cross_ref[:, place] + block_product(hi_ref, lo_ref, numbers, values)) * factor
        own_ref[:, place] = product[:rows]
        other_ref[:rows, place] = product[rows:]
        squares = (even_ref[place, :] + ring_squares(values)) + odd_ref[place, :]
        norms = lax.dot_general(
            jnp.ones((8, squares.shape[1]), jnp.float32),
            squares,
            (((1,), (1,)), ((), ())),
            precision=lax.Precision.HIGHEST,
            preferred_element_type=jnp.float32,
        )
        norm_ref[:, place] = norms
        other_ref[rows:, place] = norms


def products_call(kernel, share, operands, out_shapes):
    vmem = pl.BlockSpec(memory_space=pltpu.VMEM)
    rows, width = operands[0].shape
    return pl.pallas_call(
        kernel,
        in_specs=[vmem] * len(operands),
        out_specs=[vmem] * len(out_shapes),
        out_shape=[jax.ShapeDtypeStruct(dims, jnp.float32) for dims in out_shapes],
        compiler_params=pltpu.CompilerParams(vmem_limit_bytes=14 * 1024 * 1024),
        cost_estimate=pl.CostEstimate(
            flops=share * 6 * rows * 256 * width, bytes_accessed=share * 1024 * 1024, transcendentals=0
        ),
    )(*operands)


def near_products(parts, along_x, along_z):
    rows = parts[0].shape[0]
    _, cols, part = along_x[0].shape
    near = [v for q in (along_x, along_z) for v in (q[0], q[1], q[4])]
    return products_call(near_kernel, 3, (*parts, *near), [(rows, 2 * cols), (2 * cols, part), (2 * cols, part)])


def far_products(factor, parts, sums, along_x, along_z):
    rows = parts[0].shape[0]
    _, cols, part = along_x[0].shape
    far = [v for q in (along_x, along_z) for v in q[2:4]]
    shapes = [(rows // 2, 2 * cols), (rows // 2 + 8, 2 * cols), (8, 2 * cols)]
    return products_call(functools.partial(far_kernel, factor), 1, (*parts, *sums, *far), shapes)


def whole_split_kernel(value_ref, hi_ref, lo_ref):
    hi_ref[...], lo_ref[...] = split(value_ref[...])


def whole_split(noise):
    rows, width = noise.shape
    block = pl.BlockSpec((rows, 1024), lambda i: (0, i))
    return pl.pallas_call(
        whole_split_kernel,
        grid=(width // 1024,),
        in_specs=[block],
        out_specs=[block] * 2,
        out_shape=[jax.ShapeDtypeStruct((rows, width), jnp.bfloat16)] * 2,
        cost_estimate=pl.CostEstimate(flops=0, bytes_accessed=12 * 1024 * 1024, transcendentals=0),
    )(noise)


def finish_kernel(
    factor,
    group,
    own_ref,
    taken_ref,
    norm_ref,
    hi_hbm,
    lo_hbm,
    data_hbm,
    cross_ref,
    norms_ref,
    hi_ref,
    lo_ref,
    data_ref,
    square_ref,
    sems,
):
    rows, done = own_ref.shape
    blocks, cols, part = data_ref.shape
    depth = group * part
    copies = []
    for i in range(blocks // group):
        columns = pl.ds(i * depth, depth)
        held = pl.ds(i * group, group)
        copies.append(
            [
                pltpu.make_async_copy(data_hbm.at[held], data_ref.at[held], sems.at[i, 0]),
                pltpu.make_async_copy(hi_hbm.at[:, columns], hi_ref.at[:, columns], sems.at[i, 1]),
                pltpu.make_async_copy(lo_hbm.at[:, columns], lo_ref.at[:, columns], sems.at[i, 2]),
            ]
        )
        for copy in copies[-1]:
            copy.start()
    cross_ref[:, :done] = own_ref[...] + taken_ref[:rows, :]
    norms_ref[:, :done] = norm_ref[...] + taken_ref[rows:, :]
    for i in range(blocks // group):
        for copy in copies[i]:
            copy.wait()
        values = [data_ref[i * group + j] for j in range(group)]
        product = block_product(hi_ref, lo_ref, range(i * group, (i + 1) * group), values)
        squares = sum(v * v for v in values)
        if i == 0:
            cross_ref[:, done:] = product
            square_ref[...] = squares
        else:
            cross_ref[:, done:] += product
            square_ref[...] += squares
    cross_ref[:, done:] = cross_ref[:, done:] * factor
    norms_ref[:, done:] = lax.dot_general(
        jnp.ones((8, part), jnp.float32),
        square_ref[...],
        (((1,), (1,)), ((), ())),
        precision=lax.Precision.HIGHEST,
        preferred_element_type=jnp.float32,
    )


def finish_products(factor, parts, own, taken, norms, gathered):
    rows, width = parts[0].shape
    blocks, cols, part = gathered.shape
    total = own.shape[1] + cols
    group = 4
    vmem = pl.BlockSpec(memory_space=pltpu.VMEM)
    return pl.pallas_call(
        functools.partial(finish_kernel, factor, group),
        in_specs=[vmem] * 3 + [pl.BlockSpec(memory_space=pltpu.HBM)] * 3,
        out_specs=[vmem] * 2,
        out_shape=[
            jax.ShapeDtypeStruct((rows, total), jnp.float32),
            jax.ShapeDtypeStruct((8, total), jnp.float32),
        ],
        scratch_shapes=[
            pltpu.VMEM((rows, width), jnp.bfloat16),
            pltpu.VMEM((rows, width), jnp.bfloat16),
            pltpu.VMEM((blocks, cols, part), jnp.float32),
            pltpu.VMEM((cols, part), jnp.float32),
            pltpu.SemaphoreType.DMA((blocks // group, 3)),
        ],
        compiler_params=pltpu.CompilerParams(vmem_limit_bytes=VMEM_LIMIT),
        cost_estimate=pl.CostEstimate(
            flops=6 * rows * cols * width, bytes_accessed=4 * cols * width, transcendentals=0
        ),
    )(own, taken, norms, *parts, gathered)


def target_kernel(
    place_ref,
    noise_ref,
    data_pot_ref,
    own_ref,
    one_ref,
    two_ref,
    three_ref,
    data_hbm,
    target_ref,
    total_ref,
    data_ref,
    sums_ref,
    data_sems,
):
    place = place_ref[0]
    depth = data_ref.shape[2]
    mul = functools.partial(jnp.dot, preferred_element_type=jnp.float32)
    near = 1 + 2 * place_ref[1]
    pieces = ((own_ref, 0), (one_ref, near), (two_ref, 4 - near), (three_ref, 2))
    data_copies = []
    for step, (_, offset) in enumerate(pieces):
        for quarter in range(4):
            data_copies.append(
                pltpu.make_async_copy(
                    data_hbm.at[quarter, :, offset],
                    data_ref.at[step * 4 + quarter],
                    data_sems.at[step * 4 + quarter],
                )
            )
            data_copies[-1].start()
    for step, (score_ref, offset) in enumerate(pieces):
        folded = 0.0
        for quarter in range(4):
            copied = step * 4 + quarter
            data_copies[copied].wait()
            columns = slice(quarter * depth, (quarter + 1) * depth)
            values = jnp.concatenate([data_ref[copied, b] for b in range(data_ref.shape[1])], axis=1)
            data_hi, data_lo = split(values)
            weight = jnp.exp2(score_ref[:, columns] + noise_ref[...] + data_pot_ref[offset, :, columns])
            folded += sum(weight[:, c : c + 128] for c in range(0, depth, 128))
            w_hi, w_lo = split(weight)
            product = mul(w_hi, data_hi) + (mul(w_hi, data_lo) + mul(w_lo, data_hi))
            if copied == 0:
                target_ref[...] = product
            else:
                target_ref[...] += product
        sums_ref[lax.rem(place + 4 - offset, 4)] = folded
    total = (sums_ref[0] + sums_ref[1]) + (sums_ref[2] + sums_ref[3])
    total = jnp.sum(total, axis=1, keepdims=True)
    target_ref[...] = target_ref[...] / total
    total_ref[...] = jnp.broadcast_to(total, total_ref.shape)


def weighted_targets(place, noise_pot, data_pots, own, others, gathered):
    rows, cols = own.shape
    part = gathered.shape[-1]
    data = gathered.reshape(4, 8, 4, cols // 4, part)
    vmem, hbm = pl.BlockSpec(memory_space=pltpu.VMEM), pl.BlockSpec(memory_space=pl.ANY)
    return pl.pallas_call(
        target_kernel,
        in_specs=[pl.BlockSpec(memory_space=pltpu.SMEM)] + [vmem] * 6 + [hbm],
        out_specs=[vmem] * 2,
        out_shape=[
            jax.ShapeDtypeStruct((rows, 8 * part), jnp.float32),
            jax.ShapeDtypeStruct((rows, 128), jnp.float32),
        ],
        scratch_shapes=[
            pltpu.VMEM((16, 8, cols // 4, part), jnp.float32),
            pltpu.VMEM((4, rows, 128), jnp.float32),
            pltpu.SemaphoreType.DMA((16,)),
        ],
        compiler_params=pltpu.CompilerParams(vmem_limit_bytes=VMEM_LIMIT),
        cost_estimate=pl.CostEstimate(
            flops=24 * rows * cols * 8 * part, bytes_accessed=20 * 1024 * 1024, transcendentals=4 * rows * cols
        ),
    )(place, noise_pot, data_pots, own, *others, data)


def shift(v, by):
    return lax.ppermute(v, "col", [(i, (i + by) % 4) for i in range(4)])


def shift_z(v, by):
    return lax.ppermute(v, "row", [(i, (i + 8 * by) % 32) for i in range(32)])


def shift_x(v, by):
    return lax.ppermute(v, "row", [(i, i // 8 * 8 + (i + 2 * by) % 8) for i in range(32)])


def swap_cores(v):
    return lax.ppermute(v, "row", [(i, i ^ 1) for i in range(32)])


def gather_line(v, move):
    half = v.shape[0] // 2
    left, right = move(v, 1), move(v, 3)
    return v, left, move(left[:half], 1), move(right[half:], 3), right


def gather_plane(line, move):
    own, left, far0, far1, right = line
    return gather_line(jnp.stack([own, left, jnp.concatenate([far0, far1]), right]), move)


def shift_cores(v, by):
    pairs = []
    for i in range(32):
        step = 4 - by if i % 2 else by
        pairs += [(4 * i + y, 4 * i + (y + step) % 4) for y in range(4)]
    return lax.ppermute(v, ("row", "col"), pairs)


def around(v):
    return shift(v, 1), shift(v, 2), shift(v, 3)


def spread(v):
    return lax.all_to_all(jnp.broadcast_to(v[None], (32,) + v.shape), "row", 0, 0, tiled=True)


def pair_logsum(peaks, totals):
    peak = functools.reduce(jnp.maximum, peaks)
    scaled = [t * jnp.exp2(p - peak) for p, t in zip(peaks, totals)]
    return peak + jnp.log2((scaled[0] + scaled[2]) + (scaled[1] + scaled[3]))


def local(noise, data):
    rows, width = noise.shape
    cols, part = data.shape
    rows_all, cols_all = rows * 32, cols * 4
    log_rows, log_cols = math.log2(rows_all), math.log2(cols_all)
    place = lax.axis_index("col")
    quarter = cols // 4
    index = lax.axis_index("row")
    level, core = index // 8, index % 2

    gathered = lax.all_gather(data[PASSED:], "row", axis=0, tiled=False)
    line_x = gather_line(data[: PASSED // 2], shift_x)
    line_z = gather_line(data[PASSED // 2 : PASSED], shift_z)
    line_x, line_z, late_noise = lax.optimization_barrier((line_x, line_z, noise))
    along_x = gather_plane(line_x, shift_z)
    along_z = gather_plane(line_z, shift_x)

    spot = jnp.stack([level, index % 8 // 2, core]).astype(jnp.int32)
    parts = split_noise(spot, late_noise, swap_cores(late_noise))
    noise_norm = jnp.sum(late_noise * late_noise, axis=1) / width
    whole = whole_split(late_noise)

    blocks = data.reshape(4, quarter, part)
    held = []
    for k in range(4):
        block = lax.dynamic_index_in_dim(blocks, lax.rem(level + k, 4), 0, keepdims=False)
        held.append(shift_z(block, k) if k else block)
    held = jnp.stack(held)
    turned = []
    for k in range(4):
        block = lax.dynamic_index_in_dim(held, lax.rem(level + 8 - place - k, 4), 0, keepdims=False)
        turned.append(shift(block, k) if k else block)
    turned = jnp.concatenate(turned, axis=0)

    sums = near_products(parts, along_x, along_z)
    own, given, norms = far_products(2.0 * SCALE / width, parts, sums, along_x, along_z)
    taken = swap_cores(given)
    whole, gathered, turned, taken, noise_norm = lax.optimization_barrier(
        (whole, gathered, turned, taken, noise_norm)
    )
    scores, norms = finish_products(2.0 * SCALE / width, whole, own, taken, norms, gathered)
    data_norm = norms[0] / width

    turned = lax.all_gather(turned, "row", axis=0, tiled=False)

    shifted = scores - (data_norm * SCALE)[None, :]
    peak = jnp.max(shifted, axis=1)
    total = jnp.sum(jnp.exp2(shifted - peak[:, None]), axis=1)
    pair = jnp.stack([peak, total])
    pairs = (pair,) + around(pair)
    noise_pot = -log_rows - pair_logsum([p[0] for p in pairs], [p[1] for p in pairs])

    shifted = scores + noise_pot[:, None]
    peak = jnp.max(shifted, axis=0)
    total = jnp.sum(jnp.exp2(shifted - peak[None, :]), axis=0)
    pair = jnp.concatenate([peak, total]).reshape(16, 128)
    pair, mine = lax.optimization_barrier((pair, scores))
    one = shift_cores(mine, 1)
    pairs = spread(pair)
    pairs, one = lax.optimization_barrier((pairs, one))
    peaks, totals = pairs[:, :8].reshape(32, cols), pairs[:, 8:].reshape(32, cols)
    peak = jnp.max(peaks, axis=0)
    total = jnp.sum(totals * jnp.exp2(peaks - peak[None, :]), axis=0)
    data_pot = -log_cols - (peak + jnp.log2(total))

    for step in range(1, ITERS):
        total = jnp.sum(jnp.exp2(scores + noise_pot[:, None] + data_pot[None, :]), axis=1)
        before, across, after = around(total)
        noise_pot = noise_pot - log_rows - jnp.log2((total + across) + (before + after))
        total = jnp.sum(jnp.exp2(scores + noise_pot[:, None] + data_pot[None, :]), axis=0)
        total = total.reshape(8, 128)
        if step == 1:
            total, mine = lax.optimization_barrier((total, scores))
            two = shift_cores(mine, 3)
            totals = spread(total)
            totals, two = lax.optimization_barrier((totals, two))
        elif step == 2:
            total, one = lax.optimization_barrier((total, one))
            three = shift_cores(one, 1)
            totals = spread(total)
            totals, three = lax.optimization_barrier((totals, three))
        else:
            totals = spread(total)
        data_pot = data_pot - log_cols - jnp.log2(jnp.sum(totals, axis=0).reshape(cols))

    data_pots = jnp.stack((data_pot,) + around(data_pot))[:, None, :]
    targets, total = weighted_targets(
        jnp.stack([place, core]).astype(jnp.int32),
        noise_pot[:, None],
        data_pots,
        scores,
        (one, two, three),
        turned,
    )
    noise_pot = noise_pot - log_rows - jnp.log2(total[:, 0])
    return (targets, noise_norm + noise_pot / SCALE, data_norm + data_pot / SCALE)


def solution(mesh):
    placed = (P("row", None), P("col", "row"))
    return jax.shard_map(
        local,
        mesh=mesh,
        in_specs=placed,
        out_specs=(P("row", "col"), P("row"), P("col")),
        check_vma=False,
    )
```

```python
import functools
import math

import jax
import jax.numpy as jnp
from jax import lax
from jax.experimental import pallas as pl
from jax.experimental.pallas import tpu as pltpu
from jax.sharding import PartitionSpec as P

ITERS = 4
EPSILON = 0.02
LOG2E = 1.0 / math.log(2.0)
SCALE = LOG2E / EPSILON
VMEM_LIMIT = 40 * 1024 * 1024
PASSED = 384


def split(v):
    hi = v.astype(jnp.bfloat16)
    return hi, (v - hi.astype(jnp.float32)).astype(jnp.bfloat16)


def split_kernel(place_ref, own_hbm, other_hbm, hi_ref, lo_ref, held_ref, sems):
    rows, part = held_ref.shape[2:]
    copies = []
    for n in range(16):
        block = lax.rem(place_ref[0] + 4 - n // 4, 4) * 4 + lax.rem(place_ref[1] + 4 - n % 4, 4)
        columns = pl.ds(pl.multiple_of((block * 2 + place_ref[2]) * part, part), part)
        for i, noise in enumerate((own_hbm, other_hbm)):
            copies.append(pltpu.make_async_copy(noise.at[:, columns], held_ref.at[n, i], sems.at[n, i]))
            copies[-1].start()
    for n in range(16):
        for i in range(2):
            copies[2 * n + i].wait()
            hi, lo = split(held_ref[n, i])
            hi_ref[i * rows : (i + 1) * rows, n * part : (n + 1) * part] = hi
            lo_ref[i * rows : (i + 1) * rows, n * part : (n + 1) * part] = lo


def split_noise(place, own, other):
    rows, width = own.shape
    part = width // 32
    vmem, hbm = pl.BlockSpec(memory_space=pltpu.VMEM), pl.BlockSpec(memory_space=pltpu.HBM)
    return pl.pallas_call(
        split_kernel,
        in_specs=[pl.BlockSpec(memory_space=pltpu.SMEM), hbm, hbm],
        out_specs=[vmem] * 2,
        out_shape=[jax.ShapeDtypeStruct((2 * rows, 16 * part), jnp.bfloat16)] * 2,
        scratch_shapes=[pltpu.VMEM((16, 2, rows, part), jnp.float32), pltpu.SemaphoreType.DMA((16, 2))],
        compiler_params=pltpu.CompilerParams(vmem_limit_bytes=8 * 1024 * 1024),
        cost_estimate=pl.CostEstimate(flops=0, bytes_accessed=16 * 1024 * 1024, transcendentals=0),
    )(place, own, other)


def block_product(hi_ref, lo_ref, blocks, values):
    part = values[0].shape[1]
    pick = lambda ref: jnp.concatenate([ref[:, n * part : (n + 1) * part] for n in blocks], axis=1)
    return product(pick(hi_ref), pick(lo_ref), values)


def product(noise_hi, noise_lo, values):
    data_hi, data_lo = split(jnp.concatenate(values, axis=1))
    mul = functools.partial(
        lax.dot_general, dimension_numbers=(((1,), (1,)), ((), ())), preferred_element_type=jnp.float32
    )
    return mul(noise_hi, data_hi) + (mul(noise_hi, data_lo) + mul(noise_lo, data_hi))


def ring_squares(values):
    return (values[0] * values[0] + values[2] * values[2]) + (values[1] * values[1] + values[3] * values[3])


def block_number(first, across, along):
    return across * 4 + along if first == "x" else along * 4 + across


def near_kernel(hi_ref, lo_ref, *refs):
    cross_ref, even_ref, odd_ref = refs[6:]
    for half, (first, lines) in enumerate((("x", refs[:3]), ("z", refs[3:6]))):
        cols = lines[0].shape[1]
        place = slice(half * cols, (half + 1) * cols)
        squares = []
        for line, across in zip(lines, (0, 1, 3)):
            values = [line[n] for n in range(4)]
            numbers = [block_number(first, across, n) for n in range(4)]
            product = block_product(hi_ref, lo_ref, numbers, values)
            if across == 0:
                cross_ref[:, place] = product
            else:
                cross_ref[:, place] += product
            squares.append(ring_squares(values))
        even_ref[place, :] = squares[0]
        odd_ref[place, :] = squares[1] + squares[2]


def far_kernel(factor, hi_ref, lo_ref, cross_ref, even_ref, odd_ref, x0, x1, z0, z1, own_ref, other_ref, norm_ref):
    rows = own_ref.shape[0]
    for half, (first, refs) in enumerate((("x", (x0, x1)), ("z", (z0, z1)))):
        cols = refs[0].shape[1]
        place = slice(half * cols, (half + 1) * cols)
        values = [refs[i // 2][i % 2] for i in range(4)]
        numbers = [block_number(first, 2, i) for i in range(4)]
        product = (cross_ref[:, place] + block_product(hi_ref, lo_ref, numbers, values)) * factor
        own_ref[:, place] = product[:rows]
        other_ref[:rows, place] = product[rows:]
        squares = (even_ref[place, :] + ring_squares(values)) + odd_ref[place, :]
        norms = lax.dot_general(
            jnp.ones((8, squares.shape[1]), jnp.float32),
            squares,
            (((1,), (1,)), ((), ())),
            precision=lax.Precision.HIGHEST,
            preferred_element_type=jnp.float32,
        )
        norm_ref[:, place] = norms
        other_ref[rows:, place] = norms


def products_call(kernel, share, operands, out_shapes):
    vmem = pl.BlockSpec(memory_space=pltpu.VMEM)
    rows, width = operands[0].shape
    return pl.pallas_call(
        kernel,
        in_specs=[vmem] * len(operands),
        out_specs=[vmem] * len(out_shapes),
        out_shape=[jax.ShapeDtypeStruct(dims, jnp.float32) for dims in out_shapes],
        compiler_params=pltpu.CompilerParams(vmem_limit_bytes=14 * 1024 * 1024),
        cost_estimate=pl.CostEstimate(
            flops=share * 6 * rows * 256 * width, bytes_accessed=share * 1024 * 1024, transcendentals=0
        ),
    )(*operands)


def near_products(parts, along_x, along_z):
    rows = parts[0].shape[0]
    _, cols, part = along_x[0].shape
    near = [v for q in (along_x, along_z) for v in (q[0], q[1], q[4])]
    return products_call(near_kernel, 3, (*parts, *near), [(rows, 2 * cols), (2 * cols, part), (2 * cols, part)])


def far_products(factor, parts, sums, along_x, along_z):
    rows = parts[0].shape[0]
    _, cols, part = along_x[0].shape
    far = [v for q in (along_x, along_z) for v in q[2:4]]
    shapes = [(rows // 2, 2 * cols), (rows // 2 + 8, 2 * cols), (8, 2 * cols)]
    return products_call(functools.partial(far_kernel, factor), 1, (*parts, *sums, *far), shapes)


def finish_kernel(
    factor,
    group,
    own_ref,
    taken_ref,
    norm_ref,
    noise_ref,
    data_hbm,
    cross_ref,
    norms_ref,
    data_ref,
    square_ref,
    sems,
):
    rows, done = own_ref.shape
    blocks, cols, part = data_ref.shape
    depth = group * part
    copies = []
    for i in range(blocks // group):
        held = pl.ds(i * group, group)
        copies.append(pltpu.make_async_copy(data_hbm.at[held], data_ref.at[held], sems.at[i]))
        copies[-1].start()
    cross_ref[:, :done] = own_ref[...] + taken_ref[:rows, :]
    norms_ref[:, :done] = norm_ref[...] + taken_ref[rows:, :]
    for i in range(blocks // group):
        copies[i].wait()
        values = [data_ref[i * group + j] for j in range(group)]
        found = product(*split(noise_ref[:, i * depth : (i + 1) * depth]), values)
        squares = sum(v * v for v in values)
        if i == 0:
            cross_ref[:, done:] = found
            square_ref[...] = squares
        else:
            cross_ref[:, done:] += found
            square_ref[...] += squares
    cross_ref[:, done:] = cross_ref[:, done:] * factor
    norms_ref[:, done:] = lax.dot_general(
        jnp.ones((8, part), jnp.float32),
        square_ref[...],
        (((1,), (1,)), ((), ())),
        precision=lax.Precision.HIGHEST,
        preferred_element_type=jnp.float32,
    )


def finish_products(factor, noise, own, taken, norms, gathered):
    rows, width = noise.shape
    blocks, cols, part = gathered.shape
    total = own.shape[1] + cols
    group = 4
    vmem = pl.BlockSpec(memory_space=pltpu.VMEM)
    return pl.pallas_call(
        functools.partial(finish_kernel, factor, group),
        in_specs=[vmem] * 4 + [pl.BlockSpec(memory_space=pltpu.HBM)],
        out_specs=[vmem] * 2,
        out_shape=[
            jax.ShapeDtypeStruct((rows, total), jnp.float32),
            jax.ShapeDtypeStruct((8, total), jnp.float32),
        ],
        scratch_shapes=[
            pltpu.VMEM((blocks, cols, part), jnp.float32),
            pltpu.VMEM((cols, part), jnp.float32),
            pltpu.SemaphoreType.DMA((blocks // group,)),
        ],
        compiler_params=pltpu.CompilerParams(vmem_limit_bytes=VMEM_LIMIT),
        cost_estimate=pl.CostEstimate(
            flops=6 * rows * cols * width, bytes_accessed=4 * cols * width, transcendentals=0
        ),
    )(own, taken, norms, noise, gathered)


def target_kernel(
    place_ref,
    noise_ref,
    data_pot_ref,
    own_ref,
    one_ref,
    two_ref,
    three0_ref,
    three1_ref,
    data_hbm,
    target_ref,
    total_ref,
    data_ref,
    sums_ref,
    data_sems,
):
    place = place_ref[0]
    depth = data_ref.shape[2]
    mul = functools.partial(jnp.dot, preferred_element_type=jnp.float32)
    near = 1 + 2 * place_ref[1]
    pieces = (((own_ref,), 0), ((one_ref,), near), ((two_ref,), 4 - near), ((three0_ref, three1_ref), 2))
    data_copies = []
    for step, (_, offset) in enumerate(pieces):
        for quarter in range(4):
            data_copies.append(
                pltpu.make_async_copy(
                    data_hbm.at[quarter, :, offset],
                    data_ref.at[step * 4 + quarter],
                    data_sems.at[step * 4 + quarter],
                )
            )
            data_copies[-1].start()
    for step, (refs, offset) in enumerate(pieces):
        folded = 0.0
        for quarter in range(4):
            copied = step * 4 + quarter
            data_copies[copied].wait()
            columns = slice(quarter * depth, (quarter + 1) * depth)
            values = jnp.concatenate([data_ref[copied, b] for b in range(data_ref.shape[1])], axis=1)
            data_hi, data_lo = split(values)
            scores = jnp.concatenate([ref[:, columns] for ref in refs], axis=0)
            weight = jnp.exp2(scores + noise_ref[...] + data_pot_ref[offset, :, columns])
            folded += sum(weight[:, c : c + 128] for c in range(0, depth, 128))
            w_hi, w_lo = split(weight)
            product = mul(w_hi, data_hi) + (mul(w_hi, data_lo) + mul(w_lo, data_hi))
            if copied == 0:
                target_ref[...] = product
            else:
                target_ref[...] += product
        sums_ref[lax.rem(place + 4 - offset, 4)] = folded
    total = (sums_ref[0] + sums_ref[1]) + (sums_ref[2] + sums_ref[3])
    total = jnp.sum(total, axis=1, keepdims=True)
    target_ref[...] = target_ref[...] / total
    total_ref[...] = jnp.broadcast_to(total, total_ref.shape)


def weighted_targets(place, noise_pot, data_pots, own, others, gathered):
    rows, cols = own.shape
    part = gathered.shape[-1]
    data = gathered.reshape(4, 8, 4, cols // 4, part)
    vmem, hbm = pl.BlockSpec(memory_space=pltpu.VMEM), pl.BlockSpec(memory_space=pl.ANY)
    return pl.pallas_call(
        target_kernel,
        in_specs=[pl.BlockSpec(memory_space=pltpu.SMEM)] + [vmem] * 7 + [hbm],
        out_specs=[vmem] * 2,
        out_shape=[
            jax.ShapeDtypeStruct((rows, 8 * part), jnp.float32),
            jax.ShapeDtypeStruct((rows, 128), jnp.float32),
        ],
        scratch_shapes=[
            pltpu.VMEM((16, 8, cols // 4, part), jnp.float32),
            pltpu.VMEM((4, rows, 128), jnp.float32),
            pltpu.SemaphoreType.DMA((16,)),
        ],
        compiler_params=pltpu.CompilerParams(vmem_limit_bytes=VMEM_LIMIT),
        cost_estimate=pl.CostEstimate(
            flops=24 * rows * cols * 8 * part, bytes_accessed=20 * 1024 * 1024, transcendentals=4 * rows * cols
        ),
    )(place, noise_pot, data_pots, own, *others, data)


def shift(v, by):
    return lax.ppermute(v, "col", [(i, (i + by) % 4) for i in range(4)])


def shift_z(v, by):
    return lax.ppermute(v, "row", [(i, (i + 8 * by) % 32) for i in range(32)])


def shift_x(v, by):
    return lax.ppermute(v, "row", [(i, i // 8 * 8 + (i + 2 * by) % 8) for i in range(32)])


def swap_cores(v):
    return lax.ppermute(v, "row", [(i, i ^ 1) for i in range(32)])


def gather_line(v, move):
    half = v.shape[0] // 2
    left, right = move(v, 1), move(v, 3)
    return v, left, move(left[:half], 1), move(right[half:], 3), right


def gather_plane(line, move):
    own, left, far0, far1, right = line
    return gather_line(jnp.stack([own, left, jnp.concatenate([far0, far1]), right]), move)


def shift_cores(v, by):
    pairs = []
    for i in range(32):
        step = 4 - by if i % 2 else by
        pairs += [(4 * i + y, 4 * i + (y + step) % 4) for y in range(4)]
    return lax.ppermute(v, ("row", "col"), pairs)


def around(v):
    return shift(v, 1), shift(v, 2), shift(v, 3)


def spread(v):
    return lax.all_to_all(jnp.broadcast_to(v[None], (32,) + v.shape), "row", 0, 0, tiled=True)


def pair_logsum(peaks, totals):
    peak = functools.reduce(jnp.maximum, peaks)
    scaled = [t * jnp.exp2(p - peak) for p, t in zip(peaks, totals)]
    return peak + jnp.log2((scaled[0] + scaled[2]) + (scaled[1] + scaled[3]))


def local(noise, data):
    rows, width = noise.shape
    cols, part = data.shape
    rows_all, cols_all = rows * 32, cols * 4
    log_rows, log_cols = math.log2(rows_all), math.log2(cols_all)
    place = lax.axis_index("col")
    quarter = cols // 4
    index = lax.axis_index("row")
    level, core = index // 8, index % 2

    gathered = lax.all_gather(data[PASSED:], "row", axis=0, tiled=False)
    line_x = gather_line(data[: PASSED // 2], shift_x)
    line_z = gather_line(data[PASSED // 2 : PASSED], shift_z)
    line_x, line_z, late_noise = lax.optimization_barrier((line_x, line_z, noise))
    along_x = gather_plane(line_x, shift_z)
    along_z = gather_plane(line_z, shift_x)

    spot = jnp.stack([level, index % 8 // 2, core]).astype(jnp.int32)
    parts = split_noise(spot, late_noise, swap_cores(late_noise))
    noise_norm = jnp.sum(late_noise * late_noise, axis=1) / width

    blocks = data.reshape(4, quarter, part)
    held = []
    for k in range(4):
        block = lax.dynamic_index_in_dim(blocks, lax.rem(level + k, 4), 0, keepdims=False)
        held.append(shift_z(block, k) if k else block)
    held = jnp.stack(held)
    turned = []
    for k in range(4):
        block = lax.dynamic_index_in_dim(held, lax.rem(level + 8 - place - k, 4), 0, keepdims=False)
        turned.append(shift(block, k) if k else block)
    turned = jnp.concatenate(turned, axis=0)

    sums = near_products(parts, along_x, along_z)
    own, given, norms = far_products(2.0 * SCALE / width, parts, sums, along_x, along_z)
    taken = swap_cores(given)
    gathered, turned, taken, noise_norm = lax.optimization_barrier((gathered, turned, taken, noise_norm))
    scores, norms = finish_products(2.0 * SCALE / width, noise, own, taken, norms, gathered)
    data_norm = norms[0] / width

    turned = lax.all_gather(turned, "row", axis=0, tiled=False)

    shifted = scores - (data_norm * SCALE)[None, :]
    peak = jnp.max(shifted, axis=1)
    total = jnp.sum(jnp.exp2(shifted - peak[:, None]), axis=1)
    pair = jnp.stack([peak, total])
    pairs = (pair,) + around(pair)
    noise_pot = -log_rows - pair_logsum([p[0] for p in pairs], [p[1] for p in pairs])

    shifted = scores + noise_pot[:, None]
    peak = jnp.max(shifted, axis=0)
    total = jnp.sum(jnp.exp2(shifted - peak[None, :]), axis=0)
    pair = jnp.concatenate([peak, total]).reshape(16, 128)
    pair, mine = lax.optimization_barrier((pair, scores))
    one = shift_cores(mine, 1)
    pairs = spread(pair)
    pairs, one = lax.optimization_barrier((pairs, one))
    peaks, totals = pairs[:, :8].reshape(32, cols), pairs[:, 8:].reshape(32, cols)
    peak = jnp.max(peaks, axis=0)
    total = jnp.sum(totals * jnp.exp2(peaks - peak[None, :]), axis=0)
    data_pot = -log_cols - (peak + jnp.log2(total))

    for step in range(1, ITERS):
        total = jnp.sum(jnp.exp2(scores + noise_pot[:, None] + data_pot[None, :]), axis=1)
        before, across, after = around(total)
        noise_pot = noise_pot - log_rows - jnp.log2((total + across) + (before + after))
        total = jnp.sum(jnp.exp2(scores + noise_pot[:, None] + data_pot[None, :]), axis=0)
        total = total.reshape(8, 128)
        if step == 1:
            total, mine = lax.optimization_barrier((total, scores))
            two = shift_cores(mine, 3)
            totals = spread(total)
            totals, two = lax.optimization_barrier((totals, two))
        elif step == 2:
            total, one = lax.optimization_barrier((total, one))
            three0 = shift_cores(one[: rows // 2], 1)
            totals = spread(total)
            totals, three0 = lax.optimization_barrier((totals, three0))
        else:
            total, one = lax.optimization_barrier((total, one))
            three1 = shift_cores(one[rows // 2 :], 1)
            totals = spread(total)
        data_pot = data_pot - log_cols - jnp.log2(jnp.sum(totals, axis=0).reshape(cols))

    data_pots = jnp.stack((data_pot,) + around(data_pot))[:, None, :]
    targets, total = weighted_targets(
        jnp.stack([place, core]).astype(jnp.int32),
        noise_pot[:, None],
        data_pots,
        scores,
        (one, two, three0, three1),
        turned,
    )
    noise_pot = noise_pot - log_rows - jnp.log2(total[:, 0])
    return (targets, noise_norm + noise_pot / SCALE, data_norm + data_pot / SCALE)


def solution(mesh):
    placed = (P("row", None), P("col", "row"))
    return jax.shard_map(
        local,
        mesh=mesh,
        in_specs=placed,
        out_specs=(P("row", "col"), P("row"), P("col")),
        check_vma=False,
    )
```

```python
import functools
import math

import jax
import jax.numpy as jnp
from jax import lax
from jax.experimental import pallas as pl
from jax.experimental.pallas import tpu as pltpu
from jax.sharding import PartitionSpec as P

ITERS = 4
EPSILON = 0.02
LOG2E = 1.0 / math.log(2.0)
SCALE = LOG2E / EPSILON
VMEM_LIMIT = 40 * 1024 * 1024
PASSED = 512


def split(v):
    hi = v.astype(jnp.bfloat16)
    return hi, (v - hi.astype(jnp.float32)).astype(jnp.bfloat16)


def split_kernel(place_ref, own_hbm, other_hbm, hi_ref, lo_ref, held_ref, sems):
    rows, part = held_ref.shape[2:]
    copies = []
    for n in range(16):
        block = lax.rem(place_ref[0] + 4 - n // 4, 4) * 4 + lax.rem(place_ref[1] + 4 - n % 4, 4)
        columns = pl.ds(pl.multiple_of((block * 2 + place_ref[2]) * part, part), part)
        for i, noise in enumerate((own_hbm, other_hbm)):
            copies.append(pltpu.make_async_copy(noise.at[:, columns], held_ref.at[n, i], sems.at[n, i]))
            copies[-1].start()
    for n in range(16):
        for i in range(2):
            copies[2 * n + i].wait()
            hi, lo = split(held_ref[n, i])
            hi_ref[i * rows : (i + 1) * rows, n * part : (n + 1) * part] = hi
            lo_ref[i * rows : (i + 1) * rows, n * part : (n + 1) * part] = lo


def split_noise(place, own, other):
    rows, width = own.shape
    part = width // 32
    vmem, hbm = pl.BlockSpec(memory_space=pltpu.VMEM), pl.BlockSpec(memory_space=pltpu.HBM)
    return pl.pallas_call(
        split_kernel,
        in_specs=[pl.BlockSpec(memory_space=pltpu.SMEM), hbm, hbm],
        out_specs=[vmem] * 2,
        out_shape=[jax.ShapeDtypeStruct((2 * rows, 16 * part), jnp.bfloat16)] * 2,
        scratch_shapes=[pltpu.VMEM((16, 2, rows, part), jnp.float32), pltpu.SemaphoreType.DMA((16, 2))],
        compiler_params=pltpu.CompilerParams(vmem_limit_bytes=8 * 1024 * 1024),
        cost_estimate=pl.CostEstimate(flops=0, bytes_accessed=16 * 1024 * 1024, transcendentals=0),
    )(place, own, other)


def block_product(hi_ref, lo_ref, blocks, values):
    part = values[0].shape[1]
    pick = lambda ref: jnp.concatenate([ref[:, n * part : (n + 1) * part] for n in blocks], axis=1)
    return product(pick(hi_ref), pick(lo_ref), values)


def product(noise_hi, noise_lo, values):
    data_hi, data_lo = split(jnp.concatenate(values, axis=1))
    mul = functools.partial(
        lax.dot_general, dimension_numbers=(((1,), (1,)), ((), ())), preferred_element_type=jnp.float32
    )
    return mul(noise_hi, data_hi) + (mul(noise_hi, data_lo) + mul(noise_lo, data_hi))


def ring_squares(values):
    return (values[0] * values[0] + values[2] * values[2]) + (values[1] * values[1] + values[3] * values[3])


def block_number(first, across, along):
    return across * 4 + along if first == "x" else along * 4 + across


def near_kernel(hi_ref, lo_ref, *refs):
    cross_ref, even_ref, odd_ref = refs[6:]
    for half, (first, lines) in enumerate((("x", refs[:3]), ("z", refs[3:6]))):
        cols = lines[0].shape[1]
        place = slice(half * cols, (half + 1) * cols)
        squares = []
        for line, across in zip(lines, (0, 1, 3)):
            values = [line[n] for n in range(4)]
            numbers = [block_number(first, across, n) for n in range(4)]
            product = block_product(hi_ref, lo_ref, numbers, values)
            if across == 0:
                cross_ref[:, place] = product
            else:
                cross_ref[:, place] += product
            squares.append(ring_squares(values))
        even_ref[place, :] = squares[0]
        odd_ref[place, :] = squares[1] + squares[2]


def far_kernel(factor, hi_ref, lo_ref, cross_ref, even_ref, odd_ref, x0, x1, z0, z1, own_ref, other_ref, norm_ref):
    rows = own_ref.shape[0]
    for half, (first, refs) in enumerate((("x", (x0, x1)), ("z", (z0, z1)))):
        cols = refs[0].shape[1]
        place = slice(half * cols, (half + 1) * cols)
        values = [refs[i // 2][i % 2] for i in range(4)]
        numbers = [block_number(first, 2, i) for i in range(4)]
        product = (cross_ref[:, place] + block_product(hi_ref, lo_ref, numbers, values)) * factor
        own_ref[:, place] = product[:rows]
        other_ref[:rows, place] = product[rows:]
        squares = (even_ref[place, :] + ring_squares(values)) + odd_ref[place, :]
        norms = lax.dot_general(
            jnp.ones((8, squares.shape[1]), jnp.float32),
            squares,
            (((1,), (1,)), ((), ())),
            precision=lax.Precision.HIGHEST,
            preferred_element_type=jnp.float32,
        )
        norm_ref[:, place] = norms
        other_ref[rows:, place] = norms


def products_call(kernel, share, operands, out_shapes):
    vmem = pl.BlockSpec(memory_space=pltpu.VMEM)
    rows, width = operands[0].shape
    return pl.pallas_call(
        kernel,
        in_specs=[vmem] * len(operands),
        out_specs=[vmem] * len(out_shapes),
        out_shape=[jax.ShapeDtypeStruct(dims, jnp.float32) for dims in out_shapes],
        compiler_params=pltpu.CompilerParams(vmem_limit_bytes=14 * 1024 * 1024),
        cost_estimate=pl.CostEstimate(
            flops=share * 6 * rows * 256 * width, bytes_accessed=share * 1024 * 1024, transcendentals=0
        ),
    )(*operands)


def near_products(parts, along_x, along_z):
    rows = parts[0].shape[0]
    _, cols, part = along_x[0].shape
    near = [v for q in (along_x, along_z) for v in (q[0], q[1], q[4])]
    return products_call(near_kernel, 3, (*parts, *near), [(rows, 2 * cols), (2 * cols, part), (2 * cols, part)])


def far_products(factor, parts, sums, along_x, along_z):
    rows = parts[0].shape[0]
    _, cols, part = along_x[0].shape
    far = [v for q in (along_x, along_z) for v in q[2:4]]
    shapes = [(rows // 2, 2 * cols), (rows // 2 + 8, 2 * cols), (8, 2 * cols)]
    return products_call(functools.partial(far_kernel, factor), 1, (*parts, *sums, *far), shapes)


def finish_kernel(
    factor,
    group,
    own_ref,
    taken_ref,
    norm_ref,
    noise_ref,
    data_hbm,
    cross_ref,
    norms_ref,
    data_ref,
    square_ref,
    sems,
):
    rows, done = own_ref.shape
    blocks, cols, part = data_ref.shape
    depth = group * part
    copies = []
    for i in range(blocks // group):
        held = pl.ds(i * group, group)
        copies.append(pltpu.make_async_copy(data_hbm.at[held], data_ref.at[held], sems.at[i]))
        copies[-1].start()
    cross_ref[:, :done] = own_ref[...] + taken_ref[:rows, :]
    norms_ref[:, :done] = norm_ref[...] + taken_ref[rows:, :]
    for i in range(blocks // group):
        copies[i].wait()
        values = [data_ref[i * group + j] for j in range(group)]
        found = product(*split(noise_ref[:, i * depth : (i + 1) * depth]), values)
        squares = sum(v * v for v in values)
        if i == 0:
            cross_ref[:, done:] = found
            square_ref[...] = squares
        else:
            cross_ref[:, done:] += found
            square_ref[...] += squares
    cross_ref[:, done:] = cross_ref[:, done:] * factor
    norms_ref[:, done:] = lax.dot_general(
        jnp.ones((8, part), jnp.float32),
        square_ref[...],
        (((1,), (1,)), ((), ())),
        precision=lax.Precision.HIGHEST,
        preferred_element_type=jnp.float32,
    )


def finish_products(factor, noise, own, taken, norms, gathered):
    rows, width = noise.shape
    blocks, cols, part = gathered.shape
    total = own.shape[1] + cols
    group = 4
    vmem = pl.BlockSpec(memory_space=pltpu.VMEM)
    return pl.pallas_call(
        functools.partial(finish_kernel, factor, group),
        in_specs=[vmem] * 4 + [pl.BlockSpec(memory_space=pltpu.HBM)],
        out_specs=[vmem] * 2,
        out_shape=[
            jax.ShapeDtypeStruct((rows, total), jnp.float32),
            jax.ShapeDtypeStruct((8, total), jnp.float32),
        ],
        scratch_shapes=[
            pltpu.VMEM((blocks, cols, part), jnp.float32),
            pltpu.VMEM((cols, part), jnp.float32),
            pltpu.SemaphoreType.DMA((blocks // group,)),
        ],
        compiler_params=pltpu.CompilerParams(vmem_limit_bytes=VMEM_LIMIT),
        cost_estimate=pl.CostEstimate(
            flops=6 * rows * cols * width, bytes_accessed=4 * cols * width, transcendentals=0
        ),
    )(own, taken, norms, noise, gathered)


def target_kernel(
    place_ref,
    noise_ref,
    data_pot_ref,
    own_ref,
    one_ref,
    two_ref,
    three_ref,
    data_hbm,
    target_ref,
    total_ref,
    data_ref,
    sums_ref,
    data_sems,
):
    place = place_ref[0]
    depth = data_ref.shape[2]
    mul = functools.partial(jnp.dot, preferred_element_type=jnp.float32)
    near = 1 + 2 * place_ref[1]
    pieces = ((own_ref, 0), (one_ref, near), (two_ref, 4 - near), (three_ref, 2))
    data_copies = []
    for step, (_, offset) in enumerate(pieces):
        for quarter in range(4):
            data_copies.append(
                pltpu.make_async_copy(
                    data_hbm.at[quarter, :, offset],
                    data_ref.at[step * 4 + quarter],
                    data_sems.at[step * 4 + quarter],
                )
            )
            data_copies[-1].start()
    for step, (score_ref, offset) in enumerate(pieces):
        folded = 0.0
        for quarter in range(4):
            copied = step * 4 + quarter
            data_copies[copied].wait()
            columns = slice(quarter * depth, (quarter + 1) * depth)
            values = jnp.concatenate([data_ref[copied, b] for b in range(data_ref.shape[1])], axis=1)
            data_hi, data_lo = split(values)
            weight = jnp.exp2(score_ref[:, columns] + noise_ref[...] + data_pot_ref[offset, :, columns])
            folded += sum(weight[:, c : c + 128] for c in range(0, depth, 128))
            w_hi, w_lo = split(weight)
            product = mul(w_hi, data_hi) + (mul(w_hi, data_lo) + mul(w_lo, data_hi))
            if copied == 0:
                target_ref[...] = product
            else:
                target_ref[...] += product
        sums_ref[lax.rem(place + 4 - offset, 4)] = folded
    total = (sums_ref[0] + sums_ref[1]) + (sums_ref[2] + sums_ref[3])
    total = jnp.sum(total, axis=1, keepdims=True)
    target_ref[...] = target_ref[...] / total
    total_ref[...] = jnp.broadcast_to(total, total_ref.shape)


def weighted_targets(place, noise_pot, data_pots, own, others, gathered):
    rows, cols = own.shape
    part = gathered.shape[-1]
    data = gathered.reshape(4, 8, 4, cols // 4, part)
    vmem, hbm = pl.BlockSpec(memory_space=pltpu.VMEM), pl.BlockSpec(memory_space=pl.ANY)
    return pl.pallas_call(
        target_kernel,
        in_specs=[pl.BlockSpec(memory_space=pltpu.SMEM)] + [vmem] * 6 + [hbm],
        out_specs=[vmem] * 2,
        out_shape=[
            jax.ShapeDtypeStruct((rows, 8 * part), jnp.float32),
            jax.ShapeDtypeStruct((rows, 128), jnp.float32),
        ],
        scratch_shapes=[
            pltpu.VMEM((16, 8, cols // 4, part), jnp.float32),
            pltpu.VMEM((4, rows, 128), jnp.float32),
            pltpu.SemaphoreType.DMA((16,)),
        ],
        compiler_params=pltpu.CompilerParams(vmem_limit_bytes=VMEM_LIMIT),
        cost_estimate=pl.CostEstimate(
            flops=24 * rows * cols * 8 * part, bytes_accessed=20 * 1024 * 1024, transcendentals=4 * rows * cols
        ),
    )(place, noise_pot, data_pots, own, *others, data)


def shift(v, by):
    return lax.ppermute(v, "col", [(i, (i + by) % 4) for i in range(4)])


def shift_z(v, by):
    return lax.ppermute(v, "row", [(i, (i + 8 * by) % 32) for i in range(32)])


def shift_x(v, by):
    return lax.ppermute(v, "row", [(i, i // 8 * 8 + (i + 2 * by) % 8) for i in range(32)])


def swap_cores(v):
    return lax.ppermute(v, "row", [(i, i ^ 1) for i in range(32)])


def gather_line(v, move):
    half = v.shape[0] // 2
    left, right = move(v, 1), move(v, 3)
    return v, left, move(left[:half], 1), move(right[half:], 3), right


def gather_plane(line, move):
    own, left, far0, far1, right = line
    return gather_line(jnp.stack([own, left, jnp.concatenate([far0, far1]), right]), move)


def shift_cores(v, by):
    pairs = []
    for i in range(32):
        step = 4 - by if i % 2 else by
        pairs += [(4 * i + y, 4 * i + (y + step) % 4) for y in range(4)]
    return lax.ppermute(v, ("row", "col"), pairs)


def around(v):
    return shift(v, 1), shift(v, 2), shift(v, 3)


def spread(v):
    return lax.all_to_all(jnp.broadcast_to(v[None], (32,) + v.shape), "row", 0, 0, tiled=True)


def pair_logsum(peaks, totals):
    peak = functools.reduce(jnp.maximum, peaks)
    scaled = [t * jnp.exp2(p - peak) for p, t in zip(peaks, totals)]
    return peak + jnp.log2((scaled[0] + scaled[2]) + (scaled[1] + scaled[3]))


def local(noise, data):
    rows, width = noise.shape
    cols, part = data.shape
    rows_all, cols_all = rows * 32, cols * 4
    log_rows, log_cols = math.log2(rows_all), math.log2(cols_all)
    place = lax.axis_index("col")
    quarter = cols // 4
    index = lax.axis_index("row")
    level, core = index // 8, index % 2

    gathered = lax.all_gather(data[PASSED:], "row", axis=0, tiled=False)
    line_x = gather_line(data[: PASSED // 2], shift_x)
    line_z = gather_line(data[PASSED // 2 : PASSED], shift_z)
    line_x, line_z, late_noise = lax.optimization_barrier((line_x, line_z, noise))
    along_x = gather_plane(line_x, shift_z)
    along_z = gather_plane(line_z, shift_x)

    spot = jnp.stack([level, index % 8 // 2, core]).astype(jnp.int32)
    parts = split_noise(spot, late_noise, swap_cores(late_noise))
    noise_norm = jnp.sum(late_noise * late_noise, axis=1) / width

    blocks = data.reshape(4, quarter, part)
    held = []
    for k in range(4):
        block = lax.dynamic_index_in_dim(blocks, lax.rem(level + k, 4), 0, keepdims=False)
        held.append(shift_z(block, k) if k else block)
    held = jnp.stack(held)
    turned = []
    for k in range(4):
        block = lax.dynamic_index_in_dim(held, lax.rem(level + 8 - place - k, 4), 0, keepdims=False)
        turned.append(shift(block, k) if k else block)
    turned = jnp.concatenate(turned, axis=0)

    sums = near_products(parts, along_x, along_z)
    own, given, norms = far_products(2.0 * SCALE / width, parts, sums, along_x, along_z)
    taken = swap_cores(given)
    gathered, turned, taken, noise_norm = lax.optimization_barrier((gathered, turned, taken, noise_norm))
    scores, norms = finish_products(2.0 * SCALE / width, noise, own, taken, norms, gathered)
    data_norm = norms[0] / width

    turned = lax.all_gather(turned, "row", axis=0, tiled=False)

    shifted = scores - (data_norm * SCALE)[None, :]
    peak = jnp.max(shifted, axis=1)
    total = jnp.sum(jnp.exp2(shifted - peak[:, None]), axis=1)
    pair = jnp.stack([peak, total])
    pairs = (pair,) + around(pair)
    noise_pot = -log_rows - pair_logsum([p[0] for p in pairs], [p[1] for p in pairs])

    shifted = scores + noise_pot[:, None]
    peak = jnp.max(shifted, axis=0)
    total = jnp.sum(jnp.exp2(shifted - peak[None, :]), axis=0)
    pair = jnp.concatenate([peak, total]).reshape(16, 128)
    pair, mine = lax.optimization_barrier((pair, scores))
    one = shift_cores(mine, 1)
    pairs = spread(pair)
    pairs, one = lax.optimization_barrier((pairs, one))
    peaks, totals = pairs[:, :8].reshape(32, cols), pairs[:, 8:].reshape(32, cols)
    peak = jnp.max(peaks, axis=0)
    total = jnp.sum(totals * jnp.exp2(peaks - peak[None, :]), axis=0)
    data_pot = -log_cols - (peak + jnp.log2(total))

    for step in range(1, ITERS):
        total = jnp.sum(jnp.exp2(scores + noise_pot[:, None] + data_pot[None, :]), axis=1)
        before, across, after = around(total)
        noise_pot = noise_pot - log_rows - jnp.log2((total + across) + (before + after))
        total = jnp.sum(jnp.exp2(scores + noise_pot[:, None] + data_pot[None, :]), axis=0)
        total = total.reshape(8, 128)
        if step == 1:
            total, mine = lax.optimization_barrier((total, scores))
            two = shift_cores(mine, 3)
            totals = spread(total)
            totals, two = lax.optimization_barrier((totals, two))
        elif step == 2:
            total, one = lax.optimization_barrier((total, one))
            three = shift_cores(one, 1)
            totals = spread(total)
            totals, three = lax.optimization_barrier((totals, three))
        else:
            totals = spread(total)
        data_pot = data_pot - log_cols - jnp.log2(jnp.sum(totals, axis=0).reshape(cols))

    data_pots = jnp.stack((data_pot,) + around(data_pot))[:, None, :]
    targets, total = weighted_targets(
        jnp.stack([place, core]).astype(jnp.int32),
        noise_pot[:, None],
        data_pots,
        scores,
        (one, two, three),
        turned,
    )
    noise_pot = noise_pot - log_rows - jnp.log2(total[:, 0])
    return (targets, noise_norm + noise_pot / SCALE, data_norm + data_pot / SCALE)


def solution(mesh):
    placed = (P("row", None), P("col", "row"))
    return jax.shard_map(
        local,
        mesh=mesh,
        in_specs=placed,
        out_specs=(P("row", "col"), P("row"), P("col")),
        check_vma=False,
    )
```

```python
import functools
import math

import jax
import jax.numpy as jnp
from jax import lax
from jax.experimental import pallas as pl
from jax.experimental.pallas import tpu as pltpu
from jax.sharding import PartitionSpec as P

ITERS = 4
EPSILON = 0.02
LOG2E = 1.0 / math.log(2.0)
SCALE = LOG2E / EPSILON
VMEM_LIMIT = 40 * 1024 * 1024
PASSED = 512


def split(v):
    hi = v.astype(jnp.bfloat16)
    return hi, (v - hi.astype(jnp.float32)).astype(jnp.bfloat16)


def split_kernel(place_ref, own_hbm, other_hbm, hi_ref, lo_ref, held_ref, sems):
    rows, part = held_ref.shape[2:]
    copies = []
    for n in range(16):
        block = lax.rem(place_ref[0] + 4 - n // 4, 4) * 4 + lax.rem(place_ref[1] + 4 - n % 4, 4)
        columns = pl.ds(pl.multiple_of((block * 2 + place_ref[2]) * part, part), part)
        for i, noise in enumerate((own_hbm, other_hbm)):
            copies.append(pltpu.make_async_copy(noise.at[:, columns], held_ref.at[n, i], sems.at[n, i]))
            copies[-1].start()
    for n in range(16):
        for i in range(2):
            copies[2 * n + i].wait()
            hi, lo = split(held_ref[n, i])
            hi_ref[i * rows : (i + 1) * rows, n * part : (n + 1) * part] = hi
            lo_ref[i * rows : (i + 1) * rows, n * part : (n + 1) * part] = lo


def split_noise(place, own, other):
    rows, width = own.shape
    part = width // 32
    vmem, hbm = pl.BlockSpec(memory_space=pltpu.VMEM), pl.BlockSpec(memory_space=pltpu.HBM)
    return pl.pallas_call(
        split_kernel,
        in_specs=[pl.BlockSpec(memory_space=pltpu.SMEM), hbm, hbm],
        out_specs=[vmem] * 2,
        out_shape=[jax.ShapeDtypeStruct((2 * rows, 16 * part), jnp.bfloat16)] * 2,
        scratch_shapes=[pltpu.VMEM((16, 2, rows, part), jnp.float32), pltpu.SemaphoreType.DMA((16, 2))],
        compiler_params=pltpu.CompilerParams(vmem_limit_bytes=8 * 1024 * 1024),
        cost_estimate=pl.CostEstimate(flops=0, bytes_accessed=16 * 1024 * 1024, transcendentals=0),
    )(place, own, other)


def block_product(hi_ref, lo_ref, blocks, values):
    part = values[0].shape[1]
    pick = lambda ref: jnp.concatenate([ref[:, n * part : (n + 1) * part] for n in blocks], axis=1)
    noise_hi, noise_lo = pick(hi_ref), pick(lo_ref)
    data_hi, data_lo = split(jnp.concatenate(values, axis=1))
    mul = functools.partial(
        lax.dot_general, dimension_numbers=(((1,), (1,)), ((), ())), preferred_element_type=jnp.float32
    )
    return mul(noise_hi, data_hi) + (mul(noise_hi, data_lo) + mul(noise_lo, data_hi))


def ring_squares(values):
    return (values[0] * values[0] + values[2] * values[2]) + (values[1] * values[1] + values[3] * values[3])


def block_number(first, across, along):
    return across * 4 + along if first == "x" else along * 4 + across


def near_kernel(hi_ref, lo_ref, *refs):
    cross_ref, even_ref, odd_ref = refs[6:]
    for half, (first, lines) in enumerate((("x", refs[:3]), ("z", refs[3:6]))):
        cols = lines[0].shape[1]
        place = slice(half * cols, (half + 1) * cols)
        squares = []
        for line, across in zip(lines, (0, 1, 3)):
            values = [line[n] for n in range(4)]
            numbers = [block_number(first, across, n) for n in range(4)]
            product = block_product(hi_ref, lo_ref, numbers, values)
            if across == 0:
                cross_ref[:, place] = product
            else:
                cross_ref[:, place] += product
            squares.append(ring_squares(values))
        even_ref[place, :] = squares[0]
        odd_ref[place, :] = squares[1] + squares[2]


def far_kernel(factor, hi_ref, lo_ref, cross_ref, even_ref, odd_ref, x0, x1, z0, z1, own_ref, other_ref, norm_ref):
    rows = own_ref.shape[0]
    for half, (first, refs) in enumerate((("x", (x0, x1)), ("z", (z0, z1)))):
        cols = refs[0].shape[1]
        place = slice(half * cols, (half + 1) * cols)
        values = [refs[i // 2][i % 2] for i in range(4)]
        numbers = [block_number(first, 2, i) for i in range(4)]
        product = (cross_ref[:, place] + block_product(hi_ref, lo_ref, numbers, values)) * factor
        own_ref[:, place] = product[:rows]
        other_ref[:rows, place] = product[rows:]
        squares = (even_ref[place, :] + ring_squares(values)) + odd_ref[place, :]
        norms = lax.dot_general(
            jnp.ones((8, squares.shape[1]), jnp.float32),
            squares,
            (((1,), (1,)), ((), ())),
            precision=lax.Precision.HIGHEST,
            preferred_element_type=jnp.float32,
        )
        norm_ref[:, place] = norms
        other_ref[rows:, place] = norms


def products_call(kernel, share, operands, out_shapes):
    vmem = pl.BlockSpec(memory_space=pltpu.VMEM)
    rows, width = operands[0].shape
    return pl.pallas_call(
        kernel,
        in_specs=[vmem] * len(operands),
        out_specs=[vmem] * len(out_shapes),
        out_shape=[jax.ShapeDtypeStruct(dims, jnp.float32) for dims in out_shapes],
        compiler_params=pltpu.CompilerParams(vmem_limit_bytes=14 * 1024 * 1024),
        cost_estimate=pl.CostEstimate(
            flops=share * 6 * rows * 256 * width, bytes_accessed=share * 1024 * 1024, transcendentals=0
        ),
    )(*operands)


def near_products(parts, along_x, along_z):
    rows = parts[0].shape[0]
    _, cols, part = along_x[0].shape
    near = [v for q in (along_x, along_z) for v in (q[0], q[1], q[4])]
    return products_call(near_kernel, 3, (*parts, *near), [(rows, 2 * cols), (2 * cols, part), (2 * cols, part)])


def far_products(factor, parts, sums, along_x, along_z):
    rows = parts[0].shape[0]
    _, cols, part = along_x[0].shape
    far = [v for q in (along_x, along_z) for v in q[2:4]]
    shapes = [(rows // 2, 2 * cols), (rows // 2 + 8, 2 * cols), (8, 2 * cols)]
    return products_call(functools.partial(far_kernel, factor), 1, (*parts, *sums, *far), shapes)


def whole_split_kernel(value_ref, hi_ref, lo_ref):
    hi_ref[...], lo_ref[...] = split(value_ref[...])


def whole_split(noise):
    rows, width = noise.shape
    block = pl.BlockSpec((rows, 1024), lambda i: (0, i))
    return pl.pallas_call(
        whole_split_kernel,
        grid=(width // 1024,),
        in_specs=[block],
        out_specs=[block] * 2,
        out_shape=[jax.ShapeDtypeStruct((rows, width), jnp.bfloat16)] * 2,
        cost_estimate=pl.CostEstimate(flops=0, bytes_accessed=12 * 1024 * 1024, transcendentals=0),
    )(noise)


def finish_kernel(
    factor,
    group,
    own_ref,
    taken_ref,
    norm_ref,
    hi_hbm,
    lo_hbm,
    data_hbm,
    cross_ref,
    norms_ref,
    hi_ref,
    lo_ref,
    data_ref,
    square_ref,
    sems,
):
    rows, done = own_ref.shape
    blocks, cols, part = data_ref.shape
    depth = group * part
    copies = []
    for i in range(blocks // group):
        columns = pl.ds(i * depth, depth)
        held = pl.ds(i * group, group)
        copies.append(
            [
                pltpu.make_async_copy(data_hbm.at[held], data_ref.at[held], sems.at[i, 0]),
                pltpu.make_async_copy(hi_hbm.at[:, columns], hi_ref.at[:, columns], sems.at[i, 1]),
                pltpu.make_async_copy(lo_hbm.at[:, columns], lo_ref.at[:, columns], sems.at[i, 2]),
            ]
        )
        for copy in copies[-1]:
            copy.start()
    cross_ref[:, :done] = own_ref[...] + taken_ref[:rows, :]
    norms_ref[:, :done] = norm_ref[...] + taken_ref[rows:, :]
    for i in range(blocks // group):
        for copy in copies[i]:
            copy.wait()
        values = [data_ref[i * group + j] for j in range(group)]
        product = block_product(hi_ref, lo_ref, range(i * group, (i + 1) * group), values)
        squares = sum(v * v for v in values)
        if i == 0:
            cross_ref[:, done:] = product
            square_ref[...] = squares
        else:
            cross_ref[:, done:] += product
            square_ref[...] += squares
    cross_ref[:, done:] = cross_ref[:, done:] * factor
    norms_ref[:, done:] = lax.dot_general(
        jnp.ones((8, part), jnp.float32),
        square_ref[...],
        (((1,), (1,)), ((), ())),
        precision=lax.Precision.HIGHEST,
        preferred_element_type=jnp.float32,
    )


def finish_products(factor, parts, own, taken, norms, gathered):
    rows, width = parts[0].shape
    blocks, cols, part = gathered.shape
    total = own.shape[1] + cols
    group = 4
    vmem = pl.BlockSpec(memory_space=pltpu.VMEM)
    return pl.pallas_call(
        functools.partial(finish_kernel, factor, group),
        in_specs=[vmem] * 3 + [pl.BlockSpec(memory_space=pltpu.HBM)] * 3,
        out_specs=[vmem] * 2,
        out_shape=[
            jax.ShapeDtypeStruct((rows, total), jnp.float32),
            jax.ShapeDtypeStruct((8, total), jnp.float32),
        ],
        scratch_shapes=[
            pltpu.VMEM((rows, width), jnp.bfloat16),
            pltpu.VMEM((rows, width), jnp.bfloat16),
            pltpu.VMEM((blocks, cols, part), jnp.float32),
            pltpu.VMEM((cols, part), jnp.float32),
            pltpu.SemaphoreType.DMA((blocks // group, 3)),
        ],
        compiler_params=pltpu.CompilerParams(vmem_limit_bytes=VMEM_LIMIT),
        cost_estimate=pl.CostEstimate(
            flops=6 * rows * cols * width, bytes_accessed=4 * cols * width, transcendentals=0
        ),
    )(own, taken, norms, *parts, gathered)


def target_kernel(
    place_ref,
    noise_ref,
    data_pot_ref,
    own_ref,
    one_ref,
    two_ref,
    three0_ref,
    three1_ref,
    data_hbm,
    target_ref,
    total_ref,
    data_ref,
    sums_ref,
    data_sems,
):
    place = place_ref[0]
    depth = data_ref.shape[2]
    mul = functools.partial(jnp.dot, preferred_element_type=jnp.float32)
    near = 1 + 2 * place_ref[1]
    pieces = (((own_ref,), 0), ((one_ref,), near), ((two_ref,), 4 - near), ((three0_ref, three1_ref), 2))
    data_copies = []
    for step, (_, offset) in enumerate(pieces):
        for quarter in range(4):
            data_copies.append(
                pltpu.make_async_copy(
                    data_hbm.at[quarter, :, offset],
                    data_ref.at[step * 4 + quarter],
                    data_sems.at[step * 4 + quarter],
                )
            )
            data_copies[-1].start()
    for step, (refs, offset) in enumerate(pieces):
        folded = 0.0
        for quarter in range(4):
            copied = step * 4 + quarter
            data_copies[copied].wait()
            columns = slice(quarter * depth, (quarter + 1) * depth)
            values = jnp.concatenate([data_ref[copied, b] for b in range(data_ref.shape[1])], axis=1)
            data_hi, data_lo = split(values)
            scores = jnp.concatenate([ref[:, columns] for ref in refs], axis=0)
            weight = jnp.exp2(scores + noise_ref[...] + data_pot_ref[offset, :, columns])
            folded += sum(weight[:, c : c + 128] for c in range(0, depth, 128))
            w_hi, w_lo = split(weight)
            product = mul(w_hi, data_hi) + (mul(w_hi, data_lo) + mul(w_lo, data_hi))
            if copied == 0:
                target_ref[...] = product
            else:
                target_ref[...] += product
        sums_ref[lax.rem(place + 4 - offset, 4)] = folded
    total = (sums_ref[0] + sums_ref[1]) + (sums_ref[2] + sums_ref[3])
    total = jnp.sum(total, axis=1, keepdims=True)
    target_ref[...] = target_ref[...] / total
    total_ref[...] = jnp.broadcast_to(total, total_ref.shape)


def weighted_targets(place, noise_pot, data_pots, own, others, gathered):
    rows, cols = own.shape
    part = gathered.shape[-1]
    data = gathered.reshape(4, 8, 4, cols // 4, part)
    vmem, hbm = pl.BlockSpec(memory_space=pltpu.VMEM), pl.BlockSpec(memory_space=pl.ANY)
    return pl.pallas_call(
        target_kernel,
        in_specs=[pl.BlockSpec(memory_space=pltpu.SMEM)] + [vmem] * 7 + [hbm],
        out_specs=[vmem] * 2,
        out_shape=[
            jax.ShapeDtypeStruct((rows, 8 * part), jnp.float32),
            jax.ShapeDtypeStruct((rows, 128), jnp.float32),
        ],
        scratch_shapes=[
            pltpu.VMEM((16, 8, cols // 4, part), jnp.float32),
            pltpu.VMEM((4, rows, 128), jnp.float32),
            pltpu.SemaphoreType.DMA((16,)),
        ],
        compiler_params=pltpu.CompilerParams(vmem_limit_bytes=VMEM_LIMIT),
        cost_estimate=pl.CostEstimate(
            flops=24 * rows * cols * 8 * part, bytes_accessed=20 * 1024 * 1024, transcendentals=4 * rows * cols
        ),
    )(place, noise_pot, data_pots, own, *others, data)


def shift(v, by):
    return lax.ppermute(v, "col", [(i, (i + by) % 4) for i in range(4)])


def shift_z(v, by):
    return lax.ppermute(v, "row", [(i, (i + 8 * by) % 32) for i in range(32)])


def shift_x(v, by):
    return lax.ppermute(v, "row", [(i, i // 8 * 8 + (i + 2 * by) % 8) for i in range(32)])


def swap_cores(v):
    return lax.ppermute(v, "row", [(i, i ^ 1) for i in range(32)])


def gather_line(v, move):
    half = v.shape[0] // 2
    left, right = move(v, 1), move(v, 3)
    return v, left, move(left[:half], 1), move(right[half:], 3), right


def gather_plane(line, move):
    own, left, far0, far1, right = line
    return gather_line(jnp.stack([own, left, jnp.concatenate([far0, far1]), right]), move)


def shift_cores(v, by):
    pairs = []
    for i in range(32):
        step = 4 - by if i % 2 else by
        pairs += [(4 * i + y, 4 * i + (y + step) % 4) for y in range(4)]
    return lax.ppermute(v, ("row", "col"), pairs)


def around(v):
    return shift(v, 1), shift(v, 2), shift(v, 3)


def spread(v):
    return lax.all_to_all(jnp.broadcast_to(v[None], (32,) + v.shape), "row", 0, 0, tiled=True)


def pair_logsum(peaks, totals):
    peak = functools.reduce(jnp.maximum, peaks)
    scaled = [t * jnp.exp2(p - peak) for p, t in zip(peaks, totals)]
    return peak + jnp.log2((scaled[0] + scaled[2]) + (scaled[1] + scaled[3]))


def local(noise, data):
    rows, width = noise.shape
    cols, part = data.shape
    rows_all, cols_all = rows * 32, cols * 4
    log_rows, log_cols = math.log2(rows_all), math.log2(cols_all)
    place = lax.axis_index("col")
    quarter = cols // 4
    index = lax.axis_index("row")
    level, core = index // 8, index % 2

    gathered = lax.all_gather(data[PASSED:], "row", axis=0, tiled=False)
    line_x = gather_line(data[: PASSED // 2], shift_x)
    line_z = gather_line(data[PASSED // 2 : PASSED], shift_z)
    line_x, line_z, late_noise = lax.optimization_barrier((line_x, line_z, noise))
    along_x = gather_plane(line_x, shift_z)
    along_z = gather_plane(line_z, shift_x)

    spot = jnp.stack([level, index % 8 // 2, core]).astype(jnp.int32)
    parts = split_noise(spot, late_noise, swap_cores(late_noise))
    noise_norm = jnp.sum(late_noise * late_noise, axis=1) / width
    whole = whole_split(late_noise)

    blocks = data.reshape(4, quarter, part)
    held = []
    for k in range(4):
        block = lax.dynamic_index_in_dim(blocks, lax.rem(level + k, 4), 0, keepdims=False)
        held.append(shift_z(block, k) if k else block)
    held = jnp.stack(held)
    turned = []
    for k in range(4):
        block = lax.dynamic_index_in_dim(held, lax.rem(level + 8 - place - k, 4), 0, keepdims=False)
        turned.append(shift(block, k) if k else block)
    turned = jnp.concatenate(turned, axis=0)

    sums = near_products(parts, along_x, along_z)
    own, given, norms = far_products(2.0 * SCALE / width, parts, sums, along_x, along_z)
    taken = swap_cores(given)
    whole, gathered, turned, taken, noise_norm = lax.optimization_barrier(
        (whole, gathered, turned, taken, noise_norm)
    )
    scores, norms = finish_products(2.0 * SCALE / width, whole, own, taken, norms, gathered)
    data_norm = norms[0] / width

    turned = lax.all_gather(turned, "row", axis=0, tiled=False)

    shifted = scores - (data_norm * SCALE)[None, :]
    peak = jnp.max(shifted, axis=1)
    total = jnp.sum(jnp.exp2(shifted - peak[:, None]), axis=1)
    pair = jnp.stack([peak, total])
    pairs = (pair,) + around(pair)
    noise_pot = -log_rows - pair_logsum([p[0] for p in pairs], [p[1] for p in pairs])

    shifted = scores + noise_pot[:, None]
    peak = jnp.max(shifted, axis=0)
    total = jnp.sum(jnp.exp2(shifted - peak[None, :]), axis=0)
    pair = jnp.concatenate([peak, total]).reshape(16, 128)
    pair, mine = lax.optimization_barrier((pair, scores))
    one = shift_cores(mine, 1)
    pairs = spread(pair)
    pairs, one = lax.optimization_barrier((pairs, one))
    peaks, totals = pairs[:, :8].reshape(32, cols), pairs[:, 8:].reshape(32, cols)
    peak = jnp.max(peaks, axis=0)
    total = jnp.sum(totals * jnp.exp2(peaks - peak[None, :]), axis=0)
    data_pot = -log_cols - (peak + jnp.log2(total))

    for step in range(1, ITERS):
        total = jnp.sum(jnp.exp2(scores + noise_pot[:, None] + data_pot[None, :]), axis=1)
        before, across, after = around(total)
        noise_pot = noise_pot - log_rows - jnp.log2((total + across) + (before + after))
        total = jnp.sum(jnp.exp2(scores + noise_pot[:, None] + data_pot[None, :]), axis=0)
        total = total.reshape(8, 128)
        if step == 1:
            total, mine = lax.optimization_barrier((total, scores))
            two = shift_cores(mine, 3)
            totals = spread(total)
            totals, two = lax.optimization_barrier((totals, two))
        elif step == 2:
            total, one = lax.optimization_barrier((total, one))
            three0 = shift_cores(one[: rows // 2], 1)
            totals = spread(total)
            totals, three0 = lax.optimization_barrier((totals, three0))
        else:
            total, one = lax.optimization_barrier((total, one))
            three1 = shift_cores(one[rows // 2 :], 1)
            totals = spread(total)
        data_pot = data_pot - log_cols - jnp.log2(jnp.sum(totals, axis=0).reshape(cols))

    data_pots = jnp.stack((data_pot,) + around(data_pot))[:, None, :]
    targets, total = weighted_targets(
        jnp.stack([place, core]).astype(jnp.int32),
        noise_pot[:, None],
        data_pots,
        scores,
        (one, two, three0, three1),
        turned,
    )
    noise_pot = noise_pot - log_rows - jnp.log2(total[:, 0])
    return (targets, noise_norm + noise_pot / SCALE, data_norm + data_pot / SCALE)


def solution(mesh):
    placed = (P("row", None), P("col", "row"))
    return jax.shard_map(
        local,
        mesh=mesh,
        in_specs=placed,
        out_specs=(P("row", "col"), P("row"), P("col")),
        check_vma=False,
    )
```
